128 devices in a mesh: dom: 64 (over z_lo, x, y, core), edge: 2 (over z_hi).
Axes of the slice: x: 4, y: 4, z: 4 (z_hi: 2, z_lo: 2; z = z_hi * 2 + z_lo), core: 2. Of those that a mesh axis runs over, the one named last changes fastest.
Arguments:
- entities: bfloat16 [131072, 400], P('dom'), may hold values from -1.1953125 to 1.1953125
- relations: bfloat16 [1345, 400], replicated, may hold values from -6 to 6
- matching: int32 [64], replicated, may hold values from 0 to 63, each once
- group_counts: int32 [64, 2], P('dom'), may hold values from 1 to 6, as said below
- left_rows: int32 [64, 2, 6, 512], P('dom', None, 'edge'), may hold values from 0 to 2047
- right_rows: int32 [64, 2, 6, 512], P('dom', None, 'edge'), may hold values from 0 to 2047
- relation_ids: int32 [64, 2, 6, 512], P('dom', None, 'edge'), may hold values from 0 to 1344
- negative_rows: int32 [64, 2, 6, 1024], P('dom', None, 'edge'), may hold values from 0 to 2047
Outputs:
- entity_grad: float32 [131072, 400], P('dom')
- relation_grad: float32 [1345, 400], replicated
The draws below stay inside these ranges and needn't reach their ends.
Inputs may be any that keep to these rules, and one draw needn't show every extreme that they name: `group_counts`: live slots come first in each bucket; some bucket has all 6 slots live in every draw.
All inputs are finite; a program needn't handle non-finite values.
Results may differ from the reference program's by a relative error of at most 0.0003.
Values may be sent and summed in bfloat16 or wider, within the bound.
No kernel may reach another device: no remote copies, remote signals or barrier semaphores. Data moves between devices by JAX's collectives and lax.ppermute only.
A program may use at most 128 MiB of HBM per device.

```python
import math
import jax
import jax.numpy as jnp
import numpy as np
from jax import lax

D = 400
NREL = 1345
GROUP = 512
NEG = 1024
MAXCH = 6
ENT_DEV = 2048
PARTS_SIZE = 64
ENTITIES = 131072


def draw_group_counts(key, part):
    key = jax.random.fold_in(key, 11)
    first, second, third = jax.random.split(key, 3)
    factor_a = jax.random.randint(first, (PARTS_SIZE, 2), 1, 4)
    factor_b = jax.random.randint(second, (PARTS_SIZE, 2), 1, 4)
    counts = jnp.minimum(factor_a * factor_b, MAXCH).reshape(-1)
    picked = jax.random.randint(third, (), 0, PARTS_SIZE * 2)
    counts = jnp.where(jnp.arange(PARTS_SIZE * 2) == picked, MAXCH, counts)
    return counts.reshape(PARTS_SIZE, 2).astype(jnp.int32)


def place_ends(entries, stream_key, least, largest):
    extent = entries.shape
    spot = [jax.random.randint(jax.random.fold_in(stream_key, axis), (), 0, extent[axis]) for axis in range(len(extent))]
    entries = entries.at[tuple(spot)].set(least)
    longest = extent.index(max(extent))
    spot[longest] = (spot[longest] + 1) % extent[longest]
    return entries.at[tuple(spot)].set(largest)


def steps_of(key, extent, cuts, low, high):
    factor_of = 1.0
    for dim, blocks in cuts:
        draws = jax.random.uniform(jax.random.fold_in(jax.random.fold_in(key, 6), dim), (blocks,), jnp.float32, low / len(cuts), high / len(cuts))
        factor_of = factor_of * jnp.repeat(jnp.exp(draws), extent[dim] // blocks).reshape((-1,) + (1,) * (len(extent) - 1 - dim))
    return factor_of


def rank_bounds(count, lean):
    loads = [(1 << 20) // math.isqrt(standing ** lean) + 1 for standing in range(1, count + 1)]
    scale = 1 + sum(loads) // (1 << 30)
    return np.cumsum(np.array([max(1, weight // scale) for weight in loads]))


def ranked_ids(own_key, dims, number_of, skew):
    grid = rank_bounds(number_of, skew)
    pick = jax.random.randint(jax.random.fold_in(own_key, 1), dims, 0, int(grid[number_of - 1]))
    grade = jnp.searchsorted(jnp.asarray(grid, jnp.int32), pick, side="right")
    return jax.random.permutation(jax.random.fold_in(own_key, 2), number_of)[grade].astype(jnp.int32)


def centred(stream_key, dims, width, limit, cuts=(), kind=jnp.bfloat16):
    factor_of = steps_of(stream_key, dims, cuts, -0.22, 0.18) if cuts else 1.0
    array = jax.random.normal(stream_key, dims, jnp.float32) * width * factor_of
    return jnp.minimum(jnp.maximum(array, -limit), limit).astype(kind)


def setup_inputs(seed: int = 0) -> dict:
    arg_keys = jax.random.split(jax.random.key(seed), 9)
    entities = centred(arg_keys[0], (ENTITIES, D), 0.2, 1.1953125, ((0, 64),))
    relations = centred(arg_keys[1], (NREL, D), 1.0, 6.0)
    matching = jax.random.permutation(arg_keys[2], PARTS_SIZE).astype(jnp.int32)
    group_counts = draw_group_counts(jax.random.fold_in(arg_keys[8], 71), 0)
    left_rows = place_ends(jax.random.randint(arg_keys[4], (PARTS_SIZE, 2, MAXCH, GROUP), 0, ENT_DEV), jax.random.fold_in(arg_keys[4], 1), 0, ENT_DEV - 1).astype(jnp.int32)
    right_rows = place_ends(jax.random.randint(arg_keys[5], (PARTS_SIZE, 2, MAXCH, GROUP), 0, ENT_DEV), jax.random.fold_in(arg_keys[5], 1), 0, ENT_DEV - 1).astype(jnp.int32)
    relation_ids = place_ends(ranked_ids(arg_keys[6], (PARTS_SIZE, 2, MAXCH, GROUP), NREL, 2), jax.random.fold_in(arg_keys[6], 3), 0, NREL - 1).astype(jnp.int32)
    negative_rows = place_ends(jax.random.randint(arg_keys[7], (PARTS_SIZE, 2, MAXCH, NEG), 0, ENT_DEV), jax.random.fold_in(arg_keys[7], 1), 0, ENT_DEV - 1).astype(jnp.int32)
    return dict(entities=entities, relations=relations, matching=matching, group_counts=group_counts, left_rows=left_rows, right_rows=right_rows, relation_ids=relation_ids, negative_rows=negative_rows)


def complex_product(left, right):
    half = left.shape[-1] // 2
    a, b = left[..., :half], left[..., half:]
    c, d = right[..., :half], right[..., half:]
    return jnp.concatenate([a * c - b * d, a * d + b * c], axis=-1)


def conjugate_product(grad, right):
    half = grad.shape[-1] // 2
    a, b = grad[..., :half], grad[..., half:]
    c, d = right[..., :half], right[..., half:]
    return jnp.concatenate([a * c + b * d, b * c - a * d], axis=-1)


def group_terms(left_slab, right_slab, relations, left_idx, right_idx, rel_idx, neg_idx, weight):
    heads = left_slab[left_idx].astype(jnp.float32)
    rel = relations[rel_idx].astype(jnp.float32)
    tails = right_slab[right_idx].astype(jnp.float32)
    query = complex_product(heads, rel)
    positive = jnp.sum(query * tails, axis=-1)
    query_low = query.astype(jnp.bfloat16)
    negatives = right_slab[neg_idx]
    scores = lax.dot_general(query_low, negatives, (((1,), (1,)), ((), ())), preferred_element_type=jnp.float32)
    pos_grad = -jax.nn.sigmoid(-positive) * weight
    neg_grad = (jax.nn.sigmoid(scores) * (weight / negatives.shape[0])).astype(jnp.bfloat16)
    query_grad = pos_grad[:, None] * tails + jnp.dot(neg_grad, negatives, preferred_element_type=jnp.float32)
    tail_grad = pos_grad[:, None] * query
    neg_rows_grad = lax.dot_general(neg_grad, query_low, (((0,), (0,)), ((), ())), preferred_element_type=jnp.float32)
    head_grad = conjugate_product(query_grad, rel)
    rel_grad = conjugate_product(query_grad, heads)
    return head_grad, tail_grad, neg_rows_grad, rel_grad


def reference(entities, relations, matching, group_counts, left_rows, right_rows, relation_ids, negative_rows):
    slabs = entities.reshape(PARTS_SIZE, ENT_DEV, D)

    def per_part(carry, part_index):
        grads, rel_total = carry
        mate = matching[part_index]
        own = jnp.zeros((ENT_DEV, D), jnp.float32)
        other = jnp.zeros((ENT_DEV, D), jnp.float32)
        left_slab = slabs[part_index]
        for bucket in range(2):
            right_slab = left_slab if bucket == 0 else slabs[mate]
            for slot in range(MAXCH):
                live = (slot < group_counts[part_index, bucket]).astype(jnp.float32)
                lidx = left_rows[part_index, bucket, slot]
                ridx = right_rows[part_index, bucket, slot]
                relx = relation_ids[part_index, bucket, slot]
                nidx = negative_rows[part_index, bucket, slot]
                head_grad, tail_grad, neg_grad, rel_grad = group_terms(left_slab, right_slab, relations, lidx, ridx, relx, nidx, live)
                own = own.at[lidx].add(head_grad)
                if bucket == 0:
                    own = own.at[ridx].add(tail_grad).at[nidx].add(neg_grad)
                else:
                    other = other.at[ridx].add(tail_grad).at[nidx].add(neg_grad)
                rel_total = rel_total.at[relx].add(rel_grad)
        grads = grads.at[part_index].add(own).at[mate].add(other)
        return (grads, rel_total), None

    start = (jnp.zeros((PARTS_SIZE, ENT_DEV, D), jnp.float32), jnp.zeros((NREL, D), jnp.float32))
    (grads, rel_total), _ = lax.scan(per_part, start, jnp.arange(PARTS_SIZE, dtype=jnp.int32))
    return grads.reshape(ENTITIES, D), rel_total
```

```python
import jax
import jax.numpy as jnp
from jax import lax
from jax.experimental import pallas as pl
from jax.experimental.pallas import tpu as pltpu
from jax.sharding import PartitionSpec as P

F32 = jnp.float32
BF16 = jnp.bfloat16
CHUNK = 512
VM = pl.BlockSpec(memory_space=pltpu.VMEM)
SM = pl.BlockSpec(memory_space=pltpu.SMEM)
PARAMS = pltpu.CompilerParams(vmem_limit_bytes=58 * 2**20)

LANES = 128
SLAB_WINDOW = 112
SLAB_STARTS = (0, 96, 192, 288)
GRAD_WINDOW = 56
GRAD_STARTS = (0, 56, 112, 168, 224, 280, 336, 344)


def nn(a, b):
    return lax.dot_general(a, b, (((1,), (0,)), ((), ())), preferred_element_type=F32)


def nt(a, b):
    return lax.dot_general(a, b, (((1,), (1,)), ((), ())), preferred_element_type=F32)


def one_hot(idx, first, count):
    rows = lax.broadcasted_iota(jnp.int32, (count, idx.shape[1]), 0) + first
    return (rows == idx).astype(F32).astype(BF16)


def row_counts(idx, rows):
    high = one_hot(idx >> 7, 0, rows // LANES)
    low = one_hot(idx & (LANES - 1), 0, LANES)
    table = nt(high, low)
    return jnp.concatenate([table[i : i + 1, :] for i in range(rows // LANES)], axis=1)


def split(x):
    high = x.astype(BF16)
    return high, (x - high.astype(F32)).astype(BF16)


def sigmoid(x):
    return 1.0 / (1.0 + jnp.exp(-x))


def group(slot, left, right, by_row, relations, idx, marks, rel_marks, neg, own, other, rel_total):
    lidx, ridx, relx, nidx = [ref[slot] for ref in idx]
    edges, negatives = lidx.shape[1], nidx.shape[1]
    width, rows = left.shape
    half = width // 2
    parts = [slice(c, c + CHUNK) for c in range(0, rows, CHUNK)]
    for s in parts:
        marks[s, :edges] = one_hot(lidx, s.start, CHUNK)
        marks[s, edges:] = one_hot(ridx, s.start, CHUNK)
    rel_marks[...] = one_hot(relx, 0, relations.shape[1])
    h = nn(left[...], marks[:, :edges])
    t = nn(right[...], marks[:, edges:])
    rel = nn(relations[...], rel_marks[...])
    ha, hb, ra, rb = h[:half], h[half:], rel[:half], rel[half:]
    query = jnp.concatenate([ha * ra - hb * rb, ha * rb + hb * ra], axis=0)
    positive = jnp.sum(query * t, axis=0, keepdims=True)
    pos_grad = -sigmoid(-positive)
    query_low = query.astype(BF16)
    counts = row_counts(nidx, rows)
    for s in parts:
        scores = nn(by_row[s, :], query_low)
        neg[s, :] = (sigmoid(scores) * (1.0 / negatives)).astype(BF16)
    counted_high, counted_low = split(right[...].astype(F32) * counts)
    query_grad = pos_grad * t + nn(counted_high, neg[...]) + nn(counted_low, neg[...])
    ga, gb = query_grad[:half], query_grad[half:]
    head_high, head_low = split(jnp.concatenate([ga * ra + gb * rb, gb * ra - ga * rb], axis=0))
    rel_high, rel_low = split(jnp.concatenate([ga * ha + gb * hb, gb * ha - ga * hb], axis=0))
    tail_high, tail_low = split(pos_grad * query)
    for s in parts:
        neg_rows = nt(query_low, neg[s, :]) * counts[:, s]
        if other is None:
            both_high = jnp.concatenate([head_high, tail_high], axis=1)
            both_low = jnp.concatenate([head_low, tail_low], axis=1)
            own[:, s] += nt(both_high, marks[s, :]) + nt(both_low, marks[s, :]) + neg_rows
        else:
            own[:, s] += nt(head_high, marks[s, :edges]) + nt(head_low, marks[s, :edges])
            other[:, s] += (
                nt(tail_high, marks[s, edges:]) + nt(tail_low, marks[s, edges:]) + neg_rows
            )
    rel_total[...] += nt(rel_high, rel_marks[...]) + nt(rel_low, rel_marks[...])


def first_kernel(span, left, relations, lidx, ridx, relx, nidx, own, rel_total, by_row, marks, rel_marks, neg):
    own[...] = jnp.zeros_like(own)
    rel_total[...] = jnp.zeros_like(rel_total)
    by_row[...] = left[...].T

    def step(slot, _):
        group(slot, left, left, by_row, relations, (lidx, ridx, relx, nidx), marks, rel_marks, neg, own, None, rel_total)
        return 0

    lax.fori_loop(span[0], span[1], step, 0)


def more_kernel(span, left, relations, lidx, ridx, relx, nidx, own_in, rel_in, own, rel_total, by_row, marks, rel_marks, neg):
    own[...] = own_in[...]
    rel_total[...] = rel_in[...]
    by_row[...] = left[...].T

    def step(slot, _):
        group(slot, left, left, by_row, relations, (lidx, ridx, relx, nidx), marks, rel_marks, neg, own, None, rel_total)
        return 0

    lax.fori_loop(span[0], span[1], step, 0)


def second_kernel(
    span, left, pieces, relations, lidx, ridx, relx, nidx, own_in, rel_in,
    keep, give, other_pieces, rel_out, right, own, other, rel_total, by_row, marks, rel_marks, neg,
):
    own[...] = own_in[...]
    rel_total[...] = rel_in[...]
    other[...] = jnp.zeros_like(other)
    count = len(SLAB_STARTS)
    for j in range(pieces.shape[0]):
        lane, start = (j // count) * LANES, SLAB_STARTS[j % count]
        right[start : start + SLAB_WINDOW, lane : lane + LANES] = pieces[j]
    by_row[...] = right[...].T

    def step(slot, _):
        group(slot, left, right, by_row, relations, (lidx, ridx, relx, nidx), marks, rel_marks, neg, own, other, rel_total)
        return 0

    lax.fori_loop(0, span[1], step, 0)
    rel_out[...] = rel_total[:, : rel_out.shape[1]]
    side = span[2]
    middle = own.shape[1] // 2

    @pl.when(side == 0)
    def _():
        keep[...] = own[:, :middle]
        give[...] = own[:, middle:]

    @pl.when(side != 0)
    def _():
        keep[...] = own[:, middle:]
        give[...] = own[:, :middle]

    count = len(GRAD_STARTS)
    for j in range(other_pieces.shape[0] // 2):
        lane, start = (j // count) * LANES, GRAD_STARTS[j % count]
        for s in range(2):
            first = lane + s * middle
            other_pieces[2 * j + s] = other[start : start + GRAD_WINDOW, first : first + LANES]


def cut_kernel(slab, pieces):
    count = len(SLAB_STARTS)
    for j in range(pieces.shape[0]):
        lane, start = (j // count) * LANES, SLAB_STARTS[j % count]
        pieces[j] = slab[start : start + SLAB_WINDOW, lane : lane + LANES]


def take_kernel(matching, held, chosen):
    def step(q, _):
        chosen[q] = held[matching[q]]
        return 0

    lax.fori_loop(0, chosen.shape[0], step, 0)


def merge_kernel(matching, held, chosen):
    def step(q, _):
        chosen[matching[q]] = held[2 * q] + held[2 * q + 1]
        return 0

    lax.fori_loop(0, chosen.shape[0], step, 0)


def add_kernel(keep, got, pieces, out):
    count = len(GRAD_STARTS)
    for j in range(pieces.shape[0]):
        at = (slice(GRAD_STARTS[j % count], GRAD_STARTS[j % count] + GRAD_WINDOW), slice((j // count) * LANES, (j // count + 1) * LANES))
        out[at] = keep[at] + got[at] + pieces[j]


def join_kernel(side, mine, theirs, out):
    middle = mine.shape[1]

    @pl.when(side[0] == 0)
    def _():
        out[:, :middle] = mine[...]
        out[:, middle:] = theirs[...]

    @pl.when(side[0] != 0)
    def _():
        out[:, :middle] = theirs[...]
        out[:, middle:] = mine[...]


def call(kernel, outs, specs, scratch, *args, flops=0, moved=0):
    return pl.pallas_call(
        kernel,
        out_shape=outs,
        in_specs=specs,
        out_specs=jax.tree.map(lambda _: VM, outs),
        scratch_shapes=scratch,
        compiler_params=PARAMS,
        cost_estimate=pl.CostEstimate(flops=flops, bytes_accessed=moved, transcendentals=0),
    )(*args)


def body(entities, relations, matching, group_counts, left_rows, right_rows, relation_ids, negative_rows):
    parts = lax.axis_size("dom")
    side = lax.axis_index("edge")
    rows, width = entities.shape
    half_slots, edges = left_rows.shape[2:]
    rels = relations.shape[0]
    padded = -(-rels // LANES) * LANES
    middle = rows // 2

    slab = entities.T
    pieces = call(cut_kernel, jax.ShapeDtypeStruct((parts, SLAB_WINDOW, LANES), BF16), [VM], [], slab)
    held = lax.all_to_all(pieces, "dom", split_axis=0, concat_axis=0, tiled=True)

    rel_wide = jnp.pad(relations.T, ((0, 0), (0, padded - rels)))
    live = jnp.clip(group_counts[0] - side * half_slots, 0, half_slots).astype(jnp.int32)
    idx = [
        [ref[0, b].reshape(half_slots, 1, ref.shape[3]) for ref in (left_rows, right_rows, relation_ids, negative_rows)]
        for b in range(2)
    ]
    work = [
        pltpu.VMEM((rows, width), BF16),
        pltpu.VMEM((rows, 2 * edges), BF16),
        pltpu.VMEM((padded, edges), BF16),
        pltpu.VMEM((rows, edges), BF16),
    ]
    sums = (jax.ShapeDtypeStruct((width, rows), F32), jax.ShapeDtypeStruct((width, padded), F32))
    unit = 2 * width * rows * edges * 12
    zero = jnp.zeros((), jnp.int32)
    span_a = jnp.stack([zero, jnp.minimum(live[0], 1)])
    span_b = jnp.stack([zero + 1, live[0]])
    own, rel_total = call(first_kernel, sums, [SM] + [VM] * 6, work, span_a, slab, rel_wide, *idx[0], flops=unit)
    chosen = call(take_kernel, jax.ShapeDtypeStruct(held.shape, BF16), [SM, VM], [], matching, held)
    partner = lax.all_to_all(chosen, "dom", split_axis=0, concat_axis=0, tiled=True)
    own, rel_total = call(
        more_kernel, sums, [SM] + [VM] * 8, work, span_b, slab, rel_wide, *idx[0], own, rel_total, flops=2 * unit
    )
    span_c = jnp.stack([zero, live[1], side.astype(jnp.int32)])
    halves = jax.ShapeDtypeStruct((width, middle), F32)
    keep, give, other, rel_part = call(
        second_kernel,
        (
            halves,
            halves,
            jax.ShapeDtypeStruct((2 * parts, GRAD_WINDOW, LANES), F32),
            jax.ShapeDtypeStruct((width, rels), F32),
        ),
        [SM] + [VM] * 9,
        [
            pltpu.VMEM((width, rows), BF16),
            pltpu.VMEM((width, rows), F32),
            pltpu.VMEM((width, rows), F32),
            pltpu.VMEM((width, padded), F32),
        ]
        + work,
        span_c, slab, partner, rel_wide, *idx[1], own, rel_total,
        flops=3 * unit,
    )
    swap = [(0, 1), (1, 0)]
    relation_grad = lax.psum(rel_part, ("dom", "edge"))
    got = lax.ppermute(give, "edge", swap)
    grad_held = lax.all_to_all(other, ("dom", "edge"), split_axis=0, concat_axis=0, tiled=True)
    merged = call(
        merge_kernel, jax.ShapeDtypeStruct((parts, GRAD_WINDOW, LANES), F32), [SM, VM], [], matching, grad_held
    )
    grad_pieces = lax.all_to_all(merged, "dom", split_axis=0, concat_axis=0, tiled=True)
    mine = call(add_kernel, halves, [VM] * 3, [], keep, got, grad_pieces)
    theirs = lax.ppermute(mine, "edge", swap)
    total = call(
        join_kernel, jax.ShapeDtypeStruct((width, rows), F32), [SM, VM, VM], [], side.astype(jnp.int32)[None], mine, theirs
    )
    return total.T, relation_grad.T


def solution(mesh):
    placed = (
        P("dom", None),
        P(),
        P(),
        P("dom", None),
        P("dom", None, "edge", None),
        P("dom", None, "edge", None),
        P("dom", None, "edge", None),
        P("dom", None, "edge", None),
    )
    return jax.shard_map(
        body, mesh=mesh, in_specs=placed, out_specs=(P("dom", None), P()), check_vma=False
    )
```

```python
import jax
import jax.numpy as jnp
from jax import lax
from jax.experimental import pallas as pl
from jax.experimental.pallas import tpu as pltpu
from jax.sharding import PartitionSpec as P

F32 = jnp.float32
BF16 = jnp.bfloat16
CHUNK = 512
VM = pl.BlockSpec(memory_space=pltpu.VMEM)
SM = pl.BlockSpec(memory_space=pltpu.SMEM)
HB = pl.BlockSpec(memory_space=pl.ANY)
PARAMS = pltpu.CompilerParams(vmem_limit_bytes=58 * 2**20)

LANES = 128
SLAB_WINDOW = 112
SLAB_STARTS = (0, 96, 192, 288)
GRAD_WINDOW = 56
GRAD_STARTS = (0, 56, 112, 168, 224, 280, 336, 344)
REL_WINDOW = 144
REL_RING = 16


def nn(a, b):
    return lax.dot_general(a, b, (((1,), (0,)), ((), ())), preferred_element_type=F32)


def nt(a, b):
    return lax.dot_general(a, b, (((1,), (1,)), ((), ())), preferred_element_type=F32)


def tn(a, b):
    return lax.dot_general(a, b, (((0,), (0,)), ((), ())), preferred_element_type=F32)


def one_hot(idx, first, count):
    rows = lax.broadcasted_iota(jnp.int16, (count, idx.shape[1]), 0) + jnp.int16(first)
    return jnp.where(rows == idx.astype(jnp.int16), jnp.ones((), BF16), jnp.zeros((), BF16))


def mark(idx, out, lanes):
    for c in range(0, out.shape[0], LANES):
        out[c : c + LANES, lanes] = one_hot(idx, c, LANES)


def row_counts(idx, rows):
    high = one_hot(idx >> 7, 0, rows // LANES)
    low = one_hot(idx & (LANES - 1), 0, LANES)
    table = nt(high, low)
    return jnp.concatenate([table[i : i + 1, :] for i in range(rows // LANES)], axis=1)


def split(x):
    high = x.astype(BF16)
    return high, (x - high.astype(F32)).astype(BF16)


def sigmoid(x):
    return 1.0 / (1.0 + jnp.exp(-x))


def product(h, r):
    half = h.shape[0] // 2
    a, b, c, d = h[:half], h[half:], r[:half], r[half:]
    return jnp.concatenate([a * c - b * d, a * d + b * c], axis=0)


def conjugate(grad, r):
    half = grad.shape[0] // 2
    a, b, c, d = grad[:half], grad[half:], r[:half], r[half:]
    return jnp.concatenate([a * c + b * d, b * c - a * d], axis=0)


def columns(position, mine, bucket, idx):
    ours, theirs = idx
    slots = ours.shape[0]
    near = ours[jnp.minimum(position, slots - 1)]
    if theirs is None:
        row = near
    else:
        row = jnp.where(position < mine, near, theirs[jnp.clip(position - mine, 0, slots - 1)])
    row = row[bucket : bucket + 1]
    edges = row.shape[1] // 5
    return row[:, :edges], row[:, edges : 2 * edges], row[:, 2 * edges : 3 * edges], row[:, 3 * edges :]


def halves(off, rows):
    for c in range(0, rows // 2, CHUNK):
        yield slice(c, c + CHUNK), pl.ds(pl.multiple_of(off + c, CHUNK), CHUNK)


def negative_terms(query_low, slab, neg, negatives):
    for c in range(0, slab.shape[1], CHUNK):
        scores = tn(slab[:, c : c + CHUNK], query_low)
        neg[c : c + CHUNK, :] = (sigmoid(scores) * (1.0 / negatives)).astype(BF16)


def query_gradient(pos_grad, t, right, counts, neg):
    high, low = split(right[...].astype(F32) * counts)
    return pos_grad * t + nn(high, neg) + nn(low, neg)


def add_relations(grad, rel_marks, rel_total):
    high, low = split(grad)
    rel_total[...] += nt(high, rel_marks[...]) + nt(low, rel_marks[...])


def own_slot(position, slab, relations, idx, own, rel_total, marks, rel_marks, neg):
    lidx, ridx, relx, nidx = columns(position, 0, 0, (idx, None))
    edges, negatives = lidx.shape[1], nidx.shape[1]
    rows = slab.shape[1]
    left_lanes, right_lanes = slice(0, edges), slice(edges, 2 * edges)
    mark(lidx, marks, left_lanes)
    mark(ridx, marks, right_lanes)
    mark(relx, rel_marks, slice(0, edges))
    h = nn(slab[...], marks[:, left_lanes])
    t = nn(slab[...], marks[:, right_lanes])
    rel = nn(relations[...], rel_marks[...])
    query = product(h, rel)
    pos_grad = -sigmoid(-jnp.sum(query * t, axis=0, keepdims=True))
    query_low = query.astype(BF16)
    counts = row_counts(nidx, rows)
    negative_terms(query_low, slab, neg, negatives)
    query_grad = query_gradient(pos_grad, t, slab, counts, neg[...])
    head_high, head_low = split(conjugate(query_grad, rel))
    tail_high, tail_low = split(pos_grad * query)
    both_high = jnp.concatenate([head_high, tail_high], axis=1)
    both_low = jnp.concatenate([head_low, tail_low], axis=1)
    for c in range(0, rows, CHUNK):
        at = slice(c, c + CHUNK)
        own[:, at] += (
            nt(both_high, marks[at, :]) + nt(both_low, marks[at, :]) + nt(query_low, neg[at, :]) * counts[:, at]
        )
    add_relations(conjugate(query_grad, h), rel_marks, rel_total)


def widen(relations, rel_wide):
    rels = relations.shape[1]
    rel_wide[:, rels // LANES * LANES :] = jnp.zeros((rel_wide.shape[0], LANES), BF16)
    rel_wide[:, :rels] = relations[...]


def repeat(first, last, step):
    def run(i, _):
        step(i)
        return 0

    lax.fori_loop(first, last, run, 0)


def place(counts, slots):
    side = lax.axis_index("edge").astype(jnp.int32)
    core = (lax.axis_index("dom") % 2).astype(jnp.int32)
    every = [jnp.clip(counts[0, b], 0, 2 * slots) for b in range(2)]
    near = [jnp.clip(c - side * slots, 0, slots) for c in every]
    return side, core, near, every


def streams(refs, bufs, sems, i, out=False):
    k = lax.rem(i, 2)
    ends = [(b.at[k], r.at[i]) if out else (r.at[i], b.at[k]) for r, b in zip(refs, bufs)]
    return [pltpu.make_async_copy(a, b, sems.at[n, k]) for n, (a, b) in enumerate(ends)]


def begin(copies):
    for copy in copies:
        copy.start()


def finish(copies):
    for copy in copies:
        copy.wait()


def gather_kernel(counts, slab, relations, idx, theirs, heads, rels, weights, marks, rel_marks, rel_wide):
    _, _, near, every = place(counts, idx.shape[0])
    widen(relations, rel_wide)

    def step(i):
        lidx, _, relx, nidx = columns(i, near[1], 1, (idx, theirs))
        weights[i] = row_counts(nidx, slab.shape[1])
        mark(lidx, marks, slice(0, lidx.shape[1]))
        mark(relx, rel_marks, slice(0, relx.shape[1]))
        heads[i] = nn(slab[...], marks[...]).astype(BF16)
        rels[i] = nn(rel_wide[...], rel_marks[...]).astype(BF16)

    repeat(0, every[1], step)


def own_kernel(counts, slab, relations, idx, keep, give, rel_total, own, marks, rel_marks, neg, rel_wide):
    side, _, near, _ = place(counts, idx.shape[0])
    own[...] = jnp.zeros_like(own)
    rel_total[...] = jnp.zeros_like(rel_total)
    widen(relations, rel_wide)
    repeat(0, near[0], lambda i: own_slot(i, slab, rel_wide, idx, own, rel_total, marks, rel_marks, neg))
    middle = keep.shape[1]

    @pl.when(side == 0)
    def _():
        keep[...] = own[:, :middle]
        give[...] = own[:, middle:]

    @pl.when(side != 0)
    def _():
        keep[...] = own[:, middle:]
        give[...] = own[:, :middle]


def right_kernel(
    counts, pieces, idx, theirs, weights, heads, rels,
    other_pieces, pos_grads, right, tails, negs, other, marks, head, rel, tail, neg, in_sems, out_sems,
):
    side, _, near, every = place(counts, idx.shape[0])
    mine, total = near[1], every[1]

    def fetch(i):
        return streams((heads, rels), (head, rel), in_sems, i)

    def away(i):
        return streams((tails, negs), (tail, neg), out_sems, i, out=True)

    @pl.when(total >= 1)
    def _():
        begin(fetch(0))

    other[...] = jnp.zeros_like(other)
    count = len(SLAB_STARTS)
    for j in range(pieces.shape[0]):
        lane, start = (j // count) * LANES, SLAB_STARTS[j % count]
        right[start : start + SLAB_WINDOW, lane : lane + LANES] = pieces[j]
    rows = right.shape[1]
    off = side * (rows // 2)

    def step(i):
        @pl.when(i + 1 < total)
        def _():
            begin(fetch(i + 1))

        @pl.when(i >= 2)
        def _():
            finish(away(i - 2))

        k = lax.rem(i, 2)
        _, ridx, _, nidx = columns(i, mine, 1, (idx, theirs))
        mark(ridx, marks, slice(0, ridx.shape[1]))
        t = nn(right[...], marks[...])
        tail[k] = t.astype(BF16)
        finish(fetch(i))
        query = product(head[k].astype(F32), rel[k].astype(F32))
        pos_grad = -sigmoid(-jnp.sum(query * t, axis=0, keepdims=True))
        pos_grads[i] = pos_grad
        query_low = query.astype(BF16)
        now = neg.at[k]
        negative_terms(query_low, right, now, nidx.shape[1])
        begin(away(i))
        high, low = split(pos_grad * query)
        for to, at in halves(off, rows):
            other[:, to] += nt(high, marks[at, :]) + nt(low, marks[at, :]) + nt(query_low, now[at, :]) * weights[i, :, at]

    repeat(0, total, step)
    count = len(GRAD_STARTS)
    for j in range(other_pieces.shape[0]):
        lane, start = (j // count) * LANES, GRAD_STARTS[j % count]
        other_pieces[j] = other[start : start + GRAD_WINDOW, lane : lane + LANES]

    @pl.when(total >= 2)
    def _():
        finish(away(total - 2))

    @pl.when(total >= 1)
    def _():
        finish(away(total - 1))


def left_steps(first, last, side, mine, idx, saved, own, rel_total, marks, rel_marks, bufs, sems):
    weights, pos_grads, right, *refs = saved
    rows = right.shape[1]
    off = side * (rows // 2)

    def fetch(i):
        return streams(refs, bufs, sems, i)

    @pl.when(first < last)
    def _():
        begin(fetch(first))

    def step(i):
        @pl.when(i + 1 < last)
        def _():
            begin(fetch(i + 1))

        k = lax.rem(i, 2)
        lidx, _, relx, _ = columns(i, mine, 1, idx)
        mark(lidx, marks, slice(0, lidx.shape[1]))
        finish(fetch(i))
        rel, tail, neg = [buf[k] for buf in bufs[:3]]
        query_grad = query_gradient(pos_grads[i], tail.astype(F32), right, weights[i], neg)
        high, low = split(conjugate(query_grad, rel.astype(F32)))
        for to, at in halves(off, rows):
            own[:, to] += nt(high, marks[at, :]) + nt(low, marks[at, :])
        if rel_total is not None:
            mark(relx, rel_marks, slice(0, relx.shape[1]))
            add_relations(conjugate(query_grad, bufs[3][k].astype(F32)), rel_marks, rel_total)

    repeat(first, last, step)


def left_kernel(
    counts, idx, theirs, weights, pos_grads, right, rels, tails, negs, heads, own_in, got, rel_in,
    own, keep, give, rel_total, marks, rel_marks, rel, tail, neg, head, sems,
):
    side, core, near, _ = place(counts, idx.shape[0])
    own[...] = own_in[...] + got[...]
    rel_total[...] = rel_in[...]
    left_steps(
        0, near[1], side, near[1], (idx, theirs), (weights, pos_grads, right, rels, tails, negs, heads),
        own, rel_total, marks, rel_marks, (rel, tail, neg, head), sems,
    )
    half = rel_total.shape[0] // 2
    lanes = rel_total.shape[1] // LANES

    def cut(out, first):
        for j in range(lanes):
            out[j * half : (j + 1) * half, :] = rel_total[first : first + half, j * LANES : (j + 1) * LANES]
        out[lanes * half :, :] = jnp.zeros((out.shape[0] - lanes * half, LANES), F32)

    @pl.when(core == 0)
    def _():
        cut(keep, 0)
        cut(give, half)

    @pl.when(core != 0)
    def _():
        cut(keep, half)
        cut(give, 0)


def rest_kernel(
    counts, idx, theirs, weights, pos_grads, right, rels, tails, negs, own_in, own, marks, rel, tail, neg, sems,
):
    side, _, near, every = place(counts, idx.shape[0])
    own[...] = own_in[...]
    left_steps(
        near[1], every[1], side, near[1], (idx, theirs), (weights, pos_grads, right, rels, tails, negs),
        own, None, marks, None, (rel, tail, neg), sems,
    )


def cut_kernel(slab, pieces):
    count = len(SLAB_STARTS)
    for j in range(pieces.shape[0]):
        lane, start = (j // count) * LANES, SLAB_STARTS[j % count]
        pieces[j] = slab[start : start + SLAB_WINDOW, lane : lane + LANES]


def take_kernel(matching, held, chosen, sem):
    def step(q, _):
        pltpu.make_async_copy(held.at[matching[q]], chosen.at[q], sem).start()
        return 0

    lax.fori_loop(0, held.shape[0], step, 0)
    pltpu.make_async_copy(held, chosen, sem).wait()


def put_kernel(matching, held, chosen, sem):
    def step(q, _):
        pltpu.make_async_copy(held.at[q], chosen.at[matching[q]], sem).start()
        return 0

    lax.fori_loop(0, held.shape[0], step, 0)
    pltpu.make_async_copy(held, chosen, sem).wait()


def add_kernel(own, pieces, out):
    count = len(GRAD_STARTS)
    for j in range(pieces.shape[0]):
        first, lane = GRAD_STARTS[j % count], (j // count) * LANES
        at = (slice(first, first + GRAD_WINDOW), slice(lane, lane + LANES))
        out[at] = own[at] + pieces[j]


def join_kernel(mine, theirs, out):
    side = lax.axis_index("edge")
    middle = mine.shape[1]

    @pl.when(side == 0)
    def _():
        out[:, :middle] = mine[...]
        out[:, middle:] = theirs[...]

    @pl.when(side != 0)
    def _():
        out[:, :middle] = theirs[...]
        out[:, middle:] = mine[...]


def pair_kernel(keep, got, out):
    for j in range(out.shape[0]):
        at = slice(j * REL_WINDOW, (j + 1) * REL_WINDOW)
        out[j] = keep[at, :] + got[at, :]


def sum_kernel(held, out):
    total = held[0]
    for j in range(1, held.shape[0]):
        total = total + held[j]
    out[...] = total


def spread_kernel(a, b, c, d, out):
    total = (a[...] + b[...]) + (c[...] + d[...])
    for j in range(out.shape[0]):
        out[j] = total


def close_kernel(mine, theirs, out):
    core = lax.axis_index("dom") % 2
    half, rels = out.shape[0] // 2, out.shape[1]

    def put(ref, first):
        for j in range(-(-rels // LANES)):
            lanes = min(LANES, rels - j * LANES)
            out[first : first + half, j * LANES : j * LANES + lanes] = ref[j * half : (j + 1) * half, :lanes]

    @pl.when(core == 0)
    def _():
        put(mine, 0)
        put(theirs, half)

    @pl.when(core != 0)
    def _():
        put(mine, half)
        put(theirs, 0)


def call(kernel, outs, specs, scratch, *args, flops=0, moved=0, out_specs=None):
    return pl.pallas_call(
        kernel,
        out_shape=outs,
        in_specs=specs,
        out_specs=jax.tree.map(lambda _: VM, outs) if out_specs is None else out_specs,
        scratch_shapes=scratch,
        compiler_params=PARAMS,
        cost_estimate=pl.CostEstimate(flops=flops, bytes_accessed=moved, transcendentals=0),
    )(*args)


def shape(dims, kind=F32):
    return jax.ShapeDtypeStruct(dims, kind)


def body(entities, relations, matching, group_counts, left_rows, right_rows, relation_ids, negative_rows):
    parts = lax.axis_size("dom")
    rows, width = entities.shape
    half_slots, edges = left_rows.shape[2:]
    slots = 2 * half_slots
    rels = relations.shape[0]
    padded = -(-rels // LANES) * LANES
    middle = rows // 2
    swap = [(0, 1), (1, 0)]
    plane = 2 * REL_RING
    cores = [(i, i ^ 1) for i in range(parts)]
    planes = [(i, (i + plane) % parts) for i in range(parts)]
    corners = [(2 * i + e, 2 * ((i + plane) % parts) + 1 - e) for i in range(parts) for e in range(2)]
    rings = [[z + 2 * k + c for k in range(REL_RING)] for z in range(0, parts, plane) for c in range(2)]

    def exchange(x, groups=None):
        return lax.all_to_all(x, "dom", split_axis=0, concat_axis=0, tiled=True, axis_index_groups=groups)

    packed = jnp.concatenate(
        [jnp.swapaxes(ref[0], 0, 1) for ref in (left_rows, right_rows, relation_ids, negative_rows)], axis=2
    )
    idx = (packed, lax.ppermute(packed, "edge", swap))
    slab = entities.T
    relations = relations.T
    pieces = call(cut_kernel, shape((parts, SLAB_WINDOW, LANES), BF16), [VM], [], slab)
    pieces, idx = lax.optimization_barrier((pieces, idx))
    held = exchange(pieces)

    def mem(rows_, lanes, kind=BF16):
        return pltpu.VMEM((rows_, lanes), kind)

    one_mark, two_marks, neg = mem(rows, edges), mem(rows, 2 * edges), mem(rows, edges)
    rel_marks, rel_wide = mem(padded, edges), mem(width, padded)
    two_neg = pltpu.VMEM((2, rows, edges), BF16)
    two_wide = pltpu.VMEM((2, width, edges), BF16)
    sem = pltpu.SemaphoreType.DMA

    def sems(count):
        return sem((count, 2))

    unit = 2 * width * rows * edges
    own_shape, rel_shape = shape((width, middle)), shape((width, padded))
    gathered = shape((slots, width, edges), BF16)

    heads, rel_rows, weights = call(
        gather_kernel, (gathered, gathered, shape((slots, 1, rows))), [SM] + [VM] * 4, [one_mark, rel_marks, rel_wide],
        group_counts, slab, relations, *idx, flops=13 * unit,
    )
    held, heads = lax.optimization_barrier((held, heads))
    chosen = call(take_kernel, shape(held.shape, BF16), [SM, HB], [sem], matching, held)
    partner = exchange(chosen)
    keep, give, rel_total = call(
        own_kernel, (own_shape, own_shape, rel_shape), [SM] + [VM] * 3,
        [mem(width, rows, F32), two_marks, rel_marks, neg, rel_wide],
        group_counts, slab, relations, packed, flops=40 * unit,
    )
    got = lax.ppermute(give, "edge", swap)
    other, pos_grads, right, tails, negs = call(
        right_kernel,
        (
            shape((parts, GRAD_WINDOW, LANES)),
            shape((slots, 1, edges)),
            shape((width, rows), BF16),
            gathered,
            shape((slots, rows, edges), BF16),
        ),
        [SM] + [VM] * 4 + [HB] * 2,
        [mem(width, middle, F32), one_mark, two_wide, two_wide, two_wide, two_neg, sems(2), sems(2)],
        group_counts, partner, *idx, weights, heads, rel_rows,
        flops=30 * unit, out_specs=(VM, VM, VM, HB, HB),
    )
    grad_held = exchange(other)
    rel_flat = shape((REL_RING * REL_WINDOW, LANES))
    saved = (weights, pos_grads, right, rel_rows, tails, negs)
    own, rel_keep, rel_give = call(
        left_kernel, (own_shape, rel_flat, rel_flat), [SM] + [VM] * 5 + [HB] * 4 + [VM] * 3,
        [mem(width, padded, F32), one_mark, rel_marks, two_wide, two_wide, two_neg, two_wide, sems(4)],
        group_counts, *idx, *saved, heads, keep, got, rel_total, flops=20 * unit,
    )
    rel_got = lax.ppermute(rel_give, "dom", cores)
    grad_chosen = call(put_kernel, shape(grad_held.shape), [SM, VM], [sem], matching, grad_held, out_specs=HB)
    rel_keep, _ = lax.optimization_barrier((rel_keep, grad_chosen))
    rel_pieces = call(pair_kernel, shape((REL_RING, REL_WINDOW, LANES)), [VM, VM], [], rel_keep, rel_got)
    rel_held = exchange(rel_pieces, rings)
    rel_sum = call(sum_kernel, shape((REL_WINDOW, LANES)), [VM], [], rel_held)
    rel_held, grad_chosen = lax.optimization_barrier((rel_held, grad_chosen))
    grad_pieces = exchange(grad_chosen)
    rel_sums = [rel_sum, lax.ppermute(rel_sum, "dom", planes), lax.ppermute(rel_sum, "edge", swap)]
    rel_sums += [lax.ppermute(rel_sum, ("dom", "edge"), corners)]
    own, _ = lax.optimization_barrier((own, rel_sum))
    own = call(
        rest_kernel, own_shape, [SM] + [VM] * 5 + [HB] * 3 + [VM], [one_mark, two_wide, two_wide, two_neg, sems(3)],
        group_counts, *idx, *saved, own, flops=15 * unit,
    )
    own, grad_pieces, rel_sums = lax.optimization_barrier((own, grad_pieces, rel_sums))
    half = call(add_kernel, own_shape, [VM] * 2, [], own, grad_pieces)
    far = lax.ppermute(half, "edge", swap)
    rel_sums, half = lax.optimization_barrier((rel_sums, half))
    rel_full = call(spread_kernel, shape(rel_pieces.shape), [VM] * 4, [], *rel_sums)
    rel_mine = exchange(rel_full, rings).reshape(rel_flat.shape)
    rel_far = lax.ppermute(rel_mine, "dom", cores)
    relation_grad = call(close_kernel, shape((width, rels)), [VM, VM], [], rel_mine, rel_far)
    total = call(join_kernel, shape((width, rows)), [VM, VM], [], half, far)
    return total.T, relation_grad.T


def solution(mesh):
    placed = (
        P("dom", None),
        P(),
        P(),
        P("dom", None),
        P("dom", None, "edge", None),
        P("dom", None, "edge", None),
        P("dom", None, "edge", None),
        P("dom", None, "edge", None),
    )
    return jax.shard_map(
        body, mesh=mesh, in_specs=placed, out_specs=(P("dom", None), P()), check_vma=False
    )
```

```python
import jax
import jax.numpy as jnp
from jax import lax
from jax.experimental import pallas as pl
from jax.experimental.pallas import tpu as pltpu
from jax.sharding import PartitionSpec as P

F32 = jnp.float32
BF16 = jnp.bfloat16
CHUNK = 512
VM = pl.BlockSpec(memory_space=pltpu.VMEM)
SM = pl.BlockSpec(memory_space=pltpu.SMEM)
HB = pl.BlockSpec(memory_space=pl.ANY)
PARAMS = pltpu.CompilerParams(vmem_limit_bytes=63 * 2**20)

LANES = 128
SLAB_WINDOW = 112
SLAB_STARTS = (0, 96, 192, 288)
GRAD_WINDOW = 56
GRAD_STARTS = (0, 56, 112, 168, 224, 280, 336, 344)
REL_WINDOW = 144
REL_RING = 16


def nn(a, b):
    return lax.dot_general(a, b, (((1,), (0,)), ((), ())), preferred_element_type=F32)


def nt(a, b):
    return lax.dot_general(a, b, (((1,), (1,)), ((), ())), preferred_element_type=F32)


def tn(a, b):
    return lax.dot_general(a, b, (((0,), (0,)), ((), ())), preferred_element_type=F32)


def one_hot(idx, first, count):
    rows = lax.broadcasted_iota(jnp.int16, (count, idx.shape[1]), 0) + jnp.int16(first)
    return jnp.where(rows == idx.astype(jnp.int16), jnp.ones((), BF16), jnp.zeros((), BF16))


def mark(idx, out, lanes):
    for c in range(0, out.shape[0], LANES):
        out[c : c + LANES, lanes] = one_hot(idx, c, LANES)


def row_counts(idx, rows):
    high = one_hot(idx >> 7, 0, rows // LANES)
    low = one_hot(idx & (LANES - 1), 0, LANES)
    table = nt(high, low)
    return jnp.concatenate([table[i : i + 1, :] for i in range(rows // LANES)], axis=1)


def split(x):
    high = x.astype(BF16)
    return high, (x - high.astype(F32)).astype(BF16)


def sigmoid(x):
    return 1.0 / (1.0 + jnp.exp(-x))


def product(h, r):
    half = h.shape[0] // 2
    a, b, c, d = h[:half], h[half:], r[:half], r[half:]
    return jnp.concatenate([a * c - b * d, a * d + b * c], axis=0)


def conjugate(grad, r):
    half = grad.shape[0] // 2
    a, b, c, d = grad[:half], grad[half:], r[:half], r[half:]
    return jnp.concatenate([a * c + b * d, b * c - a * d], axis=0)


def columns(position, mine, bucket, idx):
    ours, theirs = idx
    slots = ours.shape[0]
    near = ours[jnp.minimum(position, slots - 1)]
    if theirs is None:
        row = near
    else:
        row = jnp.where(position < mine, near, theirs[jnp.clip(position - mine, 0, slots - 1)])
    row = row[bucket : bucket + 1]
    edges = row.shape[1] // 5
    return row[:, :edges], row[:, edges : 2 * edges], row[:, 2 * edges : 3 * edges], row[:, 3 * edges :]


def halves(off, rows):
    for c in range(0, rows // 2, CHUNK):
        yield slice(c, c + CHUNK), pl.ds(pl.multiple_of(off + c, CHUNK), CHUNK)


def negative_terms(query_low, slab, neg, negatives):
    for c in range(0, slab.shape[1], CHUNK):
        scores = tn(slab[:, c : c + CHUNK], query_low)
        neg[c : c + CHUNK, :] = (sigmoid(scores) * (1.0 / negatives)).astype(BF16)


def query_gradient(pos_grad, t, right, counts, neg):
    high, low = split(right[...].astype(F32) * counts)
    return pos_grad * t + nn(high, neg) + nn(low, neg)


def add_relations(grad, rel_marks, rel_total):
    high, low = split(grad)
    rel_total[...] += nt(high, rel_marks[...]) + nt(low, rel_marks[...])


def own_slot(position, slab, idx, own, rel_total, marks, rel_marks, neg, gathered):
    lidx, ridx, relx, nidx = columns(position, 0, 0, (idx, None))
    edges, negatives = lidx.shape[1], nidx.shape[1]
    rows = slab.shape[1]
    mark(lidx, marks, slice(0, edges))
    mark(ridx, marks, slice(edges, 2 * edges))
    mark(relx, rel_marks, slice(0, edges))
    h, rel, t = [x.astype(F32) for x in gathered()]
    query = product(h, rel)
    pos_grad = -sigmoid(-jnp.sum(query * t, axis=0, keepdims=True))
    query_low = query.astype(BF16)
    counts = row_counts(nidx, rows)
    negative_terms(query_low, slab, neg, negatives)
    query_grad = query_gradient(pos_grad, t, slab, counts, neg[...])
    head_high, head_low = split(conjugate(query_grad, rel))
    tail_high, tail_low = split(pos_grad * query)
    both_high = jnp.concatenate([head_high, tail_high], axis=1)
    both_low = jnp.concatenate([head_low, tail_low], axis=1)
    for c in range(0, rows, CHUNK):
        at = slice(c, c + CHUNK)
        own[:, at] += (
            nt(both_high, marks[at, :]) + nt(both_low, marks[at, :]) + nt(query_low, neg[at, :]) * counts[:, at]
        )
    add_relations(conjugate(query_grad, h), rel_marks, rel_total)


def widen(relations, rel_wide):
    rels = relations.shape[1]
    rel_wide[:, rels // LANES * LANES :] = jnp.zeros((rel_wide.shape[0], LANES), BF16)
    rel_wide[:, :rels] = relations[...]


def repeat(first, last, step):
    def run(i, _):
        step(i)
        return 0

    lax.fori_loop(first, last, run, 0)


def place(counts, slots):
    side = lax.axis_index("edge").astype(jnp.int32)
    core = (lax.axis_index("dom") % 2).astype(jnp.int32)
    every = [jnp.clip(counts[0, b], 0, 2 * slots) for b in range(2)]
    near = [jnp.clip(c - side * slots, 0, slots) for c in every]
    return side, core, near, every


def streams(refs, bufs, sems, i, out=False):
    k = lax.rem(i, 2)
    ends = [(b.at[k], r.at[i]) if out else (r.at[i], b.at[k]) for r, b in zip(refs, bufs)]
    return [pltpu.make_async_copy(a, b, sems.at[n, k]) for n, (a, b) in enumerate(ends)]


def begin(copies):
    for copy in copies:
        copy.start()


def finish(copies):
    for copy in copies:
        copy.wait()


def gather_kernel(
    counts, slab, relations, idx, theirs,
    heads, rels, weights, own_heads, own_rels, own_tails, marks, rel_marks, rel_wide,
):
    _, _, near, every = place(counts, idx.shape[0])
    widen(relations, rel_wide)

    def own_step(i):
        lidx, ridx, relx, _ = columns(i, 0, 0, (idx, None))
        mark(lidx, marks, slice(0, lidx.shape[1]))
        mark(relx, rel_marks, slice(0, relx.shape[1]))
        own_heads[i] = nn(slab[...], marks[...]).astype(BF16)
        own_rels[i] = nn(rel_wide[...], rel_marks[...]).astype(BF16)
        mark(ridx, marks, slice(0, ridx.shape[1]))
        own_tails[i] = nn(slab[...], marks[...]).astype(BF16)

    repeat(0, near[0], own_step)

    def step(i):
        lidx, _, relx, nidx = columns(i, near[1], 1, (idx, theirs))
        weights[i] = row_counts(nidx, slab.shape[1])
        mark(lidx, marks, slice(0, lidx.shape[1]))
        mark(relx, rel_marks, slice(0, relx.shape[1]))
        heads[i] = nn(slab[...], marks[...]).astype(BF16)
        rels[i] = nn(rel_wide[...], rel_marks[...]).astype(BF16)

    repeat(0, every[1], step)


def own_kernel(
    counts, slab, idx, heads, rels, tails,
    keep, give, rel_total, own, marks, rel_marks, neg, head, rel, tail, sems,
):
    side, _, near, _ = place(counts, idx.shape[0])
    last = near[0]

    def fetch(i):
        return streams((heads, rels, tails), (head, rel, tail), sems, i)

    @pl.when(last >= 1)
    def _():
        begin(fetch(0))

    own[...] = jnp.zeros_like(own)
    rel_total[...] = jnp.zeros_like(rel_total)

    def step(i):
        @pl.when(i + 1 < last)
        def _():
            begin(fetch(i + 1))

        def gathered():
            finish(fetch(i))
            return [buf[lax.rem(i, 2)] for buf in (head, rel, tail)]

        own_slot(i, slab, idx, own, rel_total, marks, rel_marks, neg, gathered)

    repeat(0, last, step)
    middle = keep.shape[1]

    @pl.when(side == 0)
    def _():
        keep[...] = own[:, :middle]
        give[...] = own[:, middle:]

    @pl.when(side != 0)
    def _():
        keep[...] = own[:, middle:]
        give[...] = own[:, :middle]


def right_kernel(
    counts, pieces, idx, theirs, weights, heads, rels,
    other_pieces, pos_grads, right, tails, negs, other, marks, head, rel, tail, neg, in_sems, out_sems,
):
    side, _, near, every = place(counts, idx.shape[0])
    mine, total = near[1], every[1]

    def fetch(i):
        return streams((heads, rels), (head, rel), in_sems, i)

    def away(i):
        return streams((tails, negs), (tail, neg), out_sems, i, out=True)

    @pl.when(total >= 1)
    def _():
        begin(fetch(0))

    other[...] = jnp.zeros_like(other)
    count = len(SLAB_STARTS)
    for j in range(pieces.shape[0]):
        lane, start = (j // count) * LANES, SLAB_STARTS[j % count]
        right[start : start + SLAB_WINDOW, lane : lane + LANES] = pieces[j]
    rows = right.shape[1]
    off = side * (rows // 2)

    def step(i):
        @pl.when(i + 1 < total)
        def _():
            begin(fetch(i + 1))

        @pl.when(i >= 2)
        def _():
            finish(away(i - 2))

        k = lax.rem(i, 2)
        _, ridx, _, nidx = columns(i, mine, 1, (idx, theirs))
        mark(ridx, marks, slice(0, ridx.shape[1]))
        t = nn(right[...], marks[...])
        tail[k] = t.astype(BF16)
        finish(fetch(i))
        query = product(head[k].astype(F32), rel[k].astype(F32))
        pos_grad = -sigmoid(-jnp.sum(query * t, axis=0, keepdims=True))
        pos_grads[i] = pos_grad
        query_low = query.astype(BF16)
        now = neg.at[k]
        negative_terms(query_low, right, now, nidx.shape[1])
        begin(away(i))
        high, low = split(pos_grad * query)
        for to, at in halves(off, rows):
            other[:, to] += nt(high, marks[at, :]) + nt(low, marks[at, :]) + nt(query_low, now[at, :]) * weights[i, :, at]

    repeat(0, total, step)
    count = len(GRAD_STARTS)
    for j in range(other_pieces.shape[0]):
        lane, start = (j // count) * LANES, GRAD_STARTS[j % count]
        other_pieces[j] = other[start : start + GRAD_WINDOW, lane : lane + LANES]

    @pl.when(total >= 2)
    def _():
        finish(away(total - 2))

    @pl.when(total >= 1)
    def _():
        finish(away(total - 1))


def left_steps(first, last, side, mine, idx, saved, own, rel_total, marks, rel_marks, bufs, sems):
    weights, pos_grads, right, *refs = saved
    rows = right.shape[1]
    off = side * (rows // 2)

    def fetch(i):
        return streams(refs, bufs, sems, i)

    @pl.when(first < last)
    def _():
        begin(fetch(first))

    def step(i):
        @pl.when(i + 1 < last)
        def _():
            begin(fetch(i + 1))

        k = lax.rem(i, 2)
        lidx, _, relx, _ = columns(i, mine, 1, idx)
        mark(lidx, marks, slice(0, lidx.shape[1]))
        finish(fetch(i))
        rel, tail, neg = [buf[k] for buf in bufs[:3]]
        query_grad = query_gradient(pos_grads[i], tail.astype(F32), right, weights[i], neg)
        high, low = split(conjugate(query_grad, rel.astype(F32)))
        for to, at in halves(off, rows):
            own[:, to] += nt(high, marks[at, :]) + nt(low, marks[at, :])
        if rel_total is not None:
            mark(relx, rel_marks, slice(0, relx.shape[1]))
            add_relations(conjugate(query_grad, bufs[3][k].astype(F32)), rel_marks, rel_total)

    repeat(first, last, step)


def left_kernel(
    counts, idx, theirs, weights, pos_grads, right, rels, tails, negs, heads, far_own, rel_in,
    own, keep, give, rel_total, marks, rel_marks, rel, tail, neg, head, sems,
):
    side, core, near, _ = place(counts, idx.shape[0])
    own[...] = jnp.zeros_like(own)
    rel_total[...] = rel_in[...]
    left_steps(
        0, near[1], side, near[1], (idx, theirs), (weights, pos_grads, right, rels, tails, negs, heads),
        own, rel_total, marks, rel_marks, (rel, tail, neg, head), sems,
    )
    half = rel_total.shape[0] // 2
    lanes = rel_total.shape[1] // LANES

    def cut(out, first):
        for j in range(lanes):
            out[j * half : (j + 1) * half, :] = rel_total[first : first + half, j * LANES : (j + 1) * LANES]
        out[lanes * half :, :] = jnp.zeros((out.shape[0] - lanes * half, LANES), F32)

    @pl.when(core == 0)
    def _():
        cut(keep, 0)
        cut(give, half)

    @pl.when(core != 0)
    def _():
        cut(keep, half)
        cut(give, 0)


def rest_kernel(
    counts, idx, theirs, weights, pos_grads, right, rels, tails, negs, own_in, near_own, far_own, own, marks, rel, tail, neg, sems,
):
    side, _, near, every = place(counts, idx.shape[0])
    own[...] = own_in[...] + (near_own[...] + far_own[...])
    left_steps(
        near[1], every[1], side, near[1], (idx, theirs), (weights, pos_grads, right, rels, tails, negs),
        own, None, marks, None, (rel, tail, neg), sems,
    )


def cut_kernel(slab, pieces):
    count = len(SLAB_STARTS)
    for j in range(pieces.shape[0]):
        lane, start = (j // count) * LANES, SLAB_STARTS[j % count]
        pieces[j] = slab[start : start + SLAB_WINDOW, lane : lane + LANES]


def take_kernel(matching, held, chosen, sem):
    def step(q, _):
        pltpu.make_async_copy(held.at[matching[q]], chosen.at[q], sem).start()
        return 0

    lax.fori_loop(0, held.shape[0], step, 0)
    pltpu.make_async_copy(held, chosen, sem).wait()


def put_kernel(matching, held, chosen, sem):
    def step(q, _):
        pltpu.make_async_copy(held.at[q], chosen.at[matching[q]], sem).start()
        return 0

    lax.fori_loop(0, held.shape[0], step, 0)
    pltpu.make_async_copy(held, chosen, sem).wait()


def add_kernel(own, pieces, first, second):
    count, cut = len(GRAD_STARTS), first.shape[0]
    for j in range(pieces.shape[0]):
        start, lane = GRAD_STARTS[j % count], (j // count) * LANES
        lanes = slice(lane, lane + LANES)
        total = own[start : start + GRAD_WINDOW, lanes] + pieces[j]
        here = max(0, min(cut - start, GRAD_WINDOW))
        if here:
            first[start : start + here, lanes] = total[:here]
        if here < GRAD_WINDOW:
            second[start + here - cut : start + GRAD_WINDOW - cut, lanes] = total[here:]


def write(parts, sems):
    copies = [pltpu.make_async_copy(a, b, sems.at[n, 0]) for n, (a, b) in enumerate(parts)]
    begin(copies)
    finish(copies)


def join_kernel(first, second, far, out, sems):
    side = lax.axis_index("edge")
    middle, cut = first.shape[1], first.shape[0]

    def put(near, away):
        write([(first, out.at[:cut, near]), (second, out.at[cut:, near]), (far, out.at[:cut, away])], sems)

    @pl.when(side == 0)
    def _():
        put(slice(0, middle), slice(middle, 2 * middle))

    @pl.when(side != 0)
    def _():
        put(slice(middle, 2 * middle), slice(0, middle))


def last_kernel(begun, far, out, sems):
    side = lax.axis_index("edge")
    middle, cut = far.shape[1], out.shape[0] - far.shape[0]

    @pl.when(side == 0)
    def _():
        write([(far, out.at[cut:, middle:])], sems)

    @pl.when(side != 0)
    def _():
        write([(far, out.at[cut:, :middle])], sems)


def pair_kernel(keep, got, out):
    for j in range(out.shape[0]):
        at = slice(j * REL_WINDOW, (j + 1) * REL_WINDOW)
        out[j] = keep[at, :] + got[at, :]


def sum_kernel(held, out):
    total = held[0]
    for j in range(1, held.shape[0]):
        total = total + held[j]
    out[...] = total


def spread_kernel(a, b, c, d, out):
    total = (a[...] + b[...]) + (c[...] + d[...])
    for j in range(out.shape[0]):
        out[j] = total


def close_kernel(mine, theirs, out):
    core = lax.axis_index("dom") % 2
    half, rels = out.shape[0] // 2, out.shape[1]

    def put(ref, first):
        for j in range(-(-rels // LANES)):
            lanes = min(LANES, rels - j * LANES)
            out[first : first + half, j * LANES : j * LANES + lanes] = ref[j * half : (j + 1) * half, :lanes]

    @pl.when(core == 0)
    def _():
        put(mine, 0)
        put(theirs, half)

    @pl.when(core != 0)
    def _():
        put(mine, half)
        put(theirs, 0)


def call(kernel, outs, specs, scratch, *args, flops=0, moved=0, out_specs=None, aliases={}):
    return pl.pallas_call(
        kernel,
        out_shape=outs,
        in_specs=specs,
        out_specs=jax.tree.map(lambda _: VM, outs) if out_specs is None else out_specs,
        scratch_shapes=scratch,
        compiler_params=PARAMS,
        input_output_aliases=aliases,
        cost_estimate=pl.CostEstimate(flops=flops, bytes_accessed=moved, transcendentals=0),
    )(*args)


def shape(dims, kind=F32):
    return jax.ShapeDtypeStruct(dims, kind)


def body(entities, relations, matching, group_counts, left_rows, right_rows, relation_ids, negative_rows):
    parts = lax.axis_size("dom")
    rows, width = entities.shape
    half_slots, edges = left_rows.shape[2:]
    slots = 2 * half_slots
    rels = relations.shape[0]
    padded = -(-rels // LANES) * LANES
    middle = rows // 2
    swap = [(0, 1), (1, 0)]
    plane = 2 * REL_RING
    cores = [(i, i ^ 1) for i in range(parts)]
    planes = [(i, (i + plane) % parts) for i in range(parts)]
    corners = [(2 * i + e, 2 * ((i + plane) % parts) + 1 - e) for i in range(parts) for e in range(2)]
    rings = [[z + 2 * k + c for k in range(REL_RING)] for z in range(0, parts, plane) for c in range(2)]

    def exchange(x, groups=None):
        return lax.all_to_all(x, "dom", split_axis=0, concat_axis=0, tiled=True, axis_index_groups=groups)

    packed = jnp.concatenate(
        [jnp.swapaxes(ref[0], 0, 1) for ref in (left_rows, right_rows, relation_ids, negative_rows)], axis=2
    )
    idx = (packed, lax.ppermute(packed, "edge", swap))
    slab = entities.T
    relations = relations.T
    pieces = call(cut_kernel, shape((parts, SLAB_WINDOW, LANES), BF16), [VM], [], slab)
    pieces, idx = lax.optimization_barrier((pieces, idx))
    held = exchange(pieces)

    def mem(rows_, lanes, kind=BF16):
        return pltpu.VMEM((rows_, lanes), kind)

    one_mark, two_marks, neg = mem(rows, edges), mem(rows, 2 * edges), mem(rows, edges)
    rel_marks, rel_wide = mem(padded, edges), mem(width, padded)
    two_neg = pltpu.VMEM((2, rows, edges), BF16)
    two_wide = pltpu.VMEM((2, width, edges), BF16)
    sem = pltpu.SemaphoreType.DMA

    def sems(count):
        return sem((count, 2))

    unit = 2 * width * rows * edges
    own_shape, rel_shape = shape((width, middle)), shape((width, padded))
    gathered = shape((slots, width, edges), BF16)

    near_gathered = shape((half_slots, width, edges), BF16)
    heads, rel_rows, weights, *own_rows = call(
        gather_kernel, (gathered, gathered, shape((slots, 1, rows))) + (near_gathered,) * 3,
        [SM] + [VM] * 4, [one_mark, rel_marks, rel_wide],
        group_counts, slab, relations, *idx, flops=22 * unit,
    )
    held, heads = lax.optimization_barrier((held, heads))
    chosen = call(take_kernel, shape(held.shape, BF16), [SM, HB], [sem], matching, held)
    partner = exchange(chosen)
    keep, give, rel_total = call(
        own_kernel, (own_shape, own_shape, rel_shape), [SM] + [VM] * 2 + [HB] * 3,
        [mem(width, rows, F32), two_marks, rel_marks, neg, two_wide, two_wide, two_wide, sems(3)],
        group_counts, slab, packed, *own_rows, flops=32 * unit,
    )
    got = lax.ppermute(give, "edge", swap)
    other, pos_grads, right, tails, negs = call(
        right_kernel,
        (
            shape((parts, GRAD_WINDOW, LANES)),
            shape((slots, 1, edges)),
            shape((width, rows), BF16),
            gathered,
            shape((slots, rows, edges), BF16),
        ),
        [SM] + [VM] * 4 + [HB] * 2,
        [mem(width, middle, F32), one_mark, two_wide, two_wide, two_wide, two_neg, sems(2), sems(2)],
        group_counts, partner, *idx, weights, heads, rel_rows,
        flops=30 * unit, out_specs=(VM, VM, VM, HB, HB),
    )
    grad_held = exchange(other)
    rel_flat = shape((REL_RING * REL_WINDOW, LANES))
    saved = (weights, pos_grads, right, rel_rows, tails, negs)
    own, rel_keep, rel_give = call(
        left_kernel, (own_shape, rel_flat, rel_flat), [SM] + [VM] * 5 + [HB] * 5 + [VM],
        [mem(width, padded, F32), one_mark, rel_marks, two_wide, two_wide, two_neg, two_wide, sems(4)],
        group_counts, *idx, *saved, heads, got, rel_total, flops=20 * unit,
    )
    rel_got = lax.ppermute(rel_give, "dom", cores)
    grad_chosen = call(put_kernel, shape(grad_held.shape), [SM, VM], [sem], matching, grad_held, out_specs=HB)
    rel_keep, _ = lax.optimization_barrier((rel_keep, grad_chosen))
    rel_pieces = call(pair_kernel, shape((REL_RING, REL_WINDOW, LANES)), [VM, VM], [], rel_keep, rel_got)
    rel_held = exchange(rel_pieces, rings)
    own, rel_pieces = lax.optimization_barrier((own, rel_pieces))
    own = call(
        rest_kernel, own_shape, [SM] + [VM] * 5 + [HB] * 3 + [VM] * 3, [one_mark, two_wide, two_wide, two_neg, sems(3)],
        group_counts, *idx, *saved, own, keep, got, flops=15 * unit,
    )
    rel_held, grad_chosen, own = lax.optimization_barrier((rel_held, grad_chosen, own))
    grad_pieces = exchange(grad_chosen)
    rel_sum = call(sum_kernel, shape((REL_WINDOW, LANES)), [VM], [], rel_held)
    rel_sums = [rel_sum, lax.ppermute(rel_sum, "dom", planes), lax.ppermute(rel_sum, "edge", swap)]
    rel_sums += [lax.ppermute(rel_sum, ("dom", "edge"), corners)]
    own, grad_pieces, rel_sums = lax.optimization_barrier((own, grad_pieces, rel_sums))
    cut = 3 * width // 32 * 8
    half_shapes = (shape((cut, middle)), shape((width - cut, middle)))
    first, second = call(add_kernel, half_shapes, [VM] * 2, [], own, grad_pieces)
    far = [lax.ppermute(x, "edge", swap) for x in (first, second)]
    rel_sums, first = lax.optimization_barrier((rel_sums, first))
    rel_full = call(spread_kernel, shape(rel_pieces.shape), [VM] * 4, [], *rel_sums)
    rel_mine = exchange(rel_full, rings).reshape(rel_flat.shape)
    rel_mine, far[0] = lax.optimization_barrier((rel_mine, far[0]))
    rel_far = lax.ppermute(rel_mine, "dom", cores)
    relation_grad = call(close_kernel, shape((width, rels)), [VM, VM], [], rel_mine, rel_far)
    whole = shape((width, rows))
    total = call(join_kernel, whole, [VM] * 3, [sems(3)], first, second, far[0], out_specs=HB)
    far[1], relation_grad = lax.optimization_barrier((far[1], relation_grad))
    total = call(last_kernel, whole, [HB, VM], [sems(1)], total, far[1], out_specs=HB, aliases={0: 0})
    return total.T, relation_grad.T


def solution(mesh):
    placed = (
        P("dom", None),
        P(),
        P(),
        P("dom", None),
        P("dom", None, "edge", None),
        P("dom", None, "edge", None),
        P("dom", None, "edge", None),
        P("dom", None, "edge", None),
    )
    return jax.shard_map(
        body, mesh=mesh, in_specs=placed, out_specs=(P("dom", None), P()), check_vma=False
    )
```

```python
import jax
import jax.numpy as jnp
from jax import lax
from jax.experimental import pallas as pl
from jax.experimental.pallas import tpu as pltpu
from jax.sharding import PartitionSpec as P

F32 = jnp.float32
BF16 = jnp.bfloat16
CHUNK = 512
VM = pl.BlockSpec(memory_space=pltpu.VMEM)
SM = pl.BlockSpec(memory_space=pltpu.SMEM)
HB = pl.BlockSpec(memory_space=pl.ANY)
PARAMS = pltpu.CompilerParams(vmem_limit_bytes=63 * 2**20)

LANES = 128
SLAB_WINDOW = 112
SLAB_STARTS = (0, 96, 192, 288)
GRAD_WINDOW = 56
GRAD_STARTS = (0, 56, 112, 168, 224, 280, 336, 344)
EARLY_ROWS = 168
REL_WINDOW = 144
REL_RING = 16


def nn(a, b):
    return lax.dot_general(a, b, (((1,), (0,)), ((), ())), preferred_element_type=F32)


def nt(a, b):
    return lax.dot_general(a, b, (((1,), (1,)), ((), ())), preferred_element_type=F32)


def tn(a, b):
    return lax.dot_general(a, b, (((0,), (0,)), ((), ())), preferred_element_type=F32)


def one_hot(idx, first, count):
    rows = lax.broadcasted_iota(jnp.int16, (count, idx.shape[1]), 0) + jnp.int16(first)
    return jnp.where(rows == idx.astype(jnp.int16), jnp.ones((), BF16), jnp.zeros((), BF16))


def mark(idx, out, lanes):
    for c in range(0, out.shape[0], LANES):
        out[c : c + LANES, lanes] = one_hot(idx, c, LANES)


def row_counts(idx, rows):
    high = one_hot(idx >> 7, 0, rows // LANES)
    low = one_hot(idx & (LANES - 1), 0, LANES)
    table = nt(high, low)
    return jnp.concatenate([table[i : i + 1, :] for i in range(rows // LANES)], axis=1)


def split(x):
    high = x.astype(BF16)
    return high, (x - high.astype(F32)).astype(BF16)


def sigmoid(x):
    return 1.0 / (1.0 + jnp.exp(-x))


def product(h, r):
    half = h.shape[0] // 2
    a, b, c, d = h[:half], h[half:], r[:half], r[half:]
    return jnp.concatenate([a * c - b * d, a * d + b * c], axis=0)


def conjugate(grad, r):
    half = grad.shape[0] // 2
    a, b, c, d = grad[:half], grad[half:], r[:half], r[half:]
    return jnp.concatenate([a * c + b * d, b * c - a * d], axis=0)


def columns(position, mine, bucket, idx):
    ours, theirs = idx
    slots = ours.shape[0]
    near = ours[jnp.minimum(position, slots - 1)]
    if theirs is None:
        row = near
    else:
        row = jnp.where(position < mine, near, theirs[jnp.clip(position - mine, 0, slots - 1)])
    row = row[bucket : bucket + 1]
    edges = row.shape[1] // 5
    return row[:, :edges], row[:, edges : 2 * edges], row[:, 2 * edges : 3 * edges], row[:, 3 * edges :]


def halves(off, rows):
    for c in range(0, rows // 2, CHUNK):
        yield slice(c, c + CHUNK), pl.ds(pl.multiple_of(off + c, CHUNK), CHUNK)


def negative_terms(query_low, slab, neg, negatives):
    for c in range(0, slab.shape[1], CHUNK):
        scores = tn(slab[:, c : c + CHUNK], query_low)
        neg[c : c + CHUNK, :] = (sigmoid(scores) * (1.0 / negatives)).astype(BF16)


def query_gradient(pos_grad, t, right, counts, neg):
    high, low = split(right[...].astype(F32) * counts)
    return pos_grad * t + nn(high, neg) + nn(low, neg)


def add_relations(grad, rel_marks, rel_total):
    high, low = split(grad)
    rel_total[...] += nt(high, rel_marks[...]) + nt(low, rel_marks[...])


def own_slot(position, slab, idx, own, rel_total, marks, rel_marks, neg, gathered):
    lidx, ridx, relx, nidx = columns(position, 0, 0, (idx, None))
    edges, negatives = lidx.shape[1], nidx.shape[1]
    rows = slab.shape[1]
    mark(lidx, marks, slice(0, edges))
    mark(ridx, marks, slice(edges, 2 * edges))
    mark(relx, rel_marks, slice(0, edges))
    h, rel, t = [x.astype(F32) for x in gathered()]
    query = product(h, rel)
    pos_grad = -sigmoid(-jnp.sum(query * t, axis=0, keepdims=True))
    query_low = query.astype(BF16)
    counts = row_counts(nidx, rows)
    negative_terms(query_low, slab, neg, negatives)
    query_grad = query_gradient(pos_grad, t, slab, counts, neg[...])
    head_high, head_low = split(conjugate(query_grad, rel))
    tail_high, tail_low = split(pos_grad * query)
    both_high = jnp.concatenate([head_high, tail_high], axis=1)
    both_low = jnp.concatenate([head_low, tail_low], axis=1)
    for c in range(0, rows, CHUNK):
        at = slice(c, c + CHUNK)
        own[:, at] += (
            nt(both_high, marks[at, :]) + nt(both_low, marks[at, :]) + nt(query_low, neg[at, :]) * counts[:, at]
        )
    add_relations(conjugate(query_grad, h), rel_marks, rel_total)


def widen(relations, rel_wide):
    rels = relations.shape[1]
    rel_wide[:, rels // LANES * LANES :] = jnp.zeros((rel_wide.shape[0], LANES), BF16)
    rel_wide[:, :rels] = relations[...]


def repeat(first, last, step):
    def run(i, _):
        step(i)
        return 0

    lax.fori_loop(first, last, run, 0)


def place(counts, slots):
    side = lax.axis_index("edge").astype(jnp.int32)
    core = (lax.axis_index("dom") % 2).astype(jnp.int32)
    every = [jnp.clip(counts[0, b], 0, 2 * slots) for b in range(2)]
    near = [jnp.clip(c - side * slots, 0, slots) for c in every]
    return side, core, near, every


def streams(refs, bufs, sems, i, out=False):
    k = lax.rem(i, 2)
    ends = [(b.at[k], r.at[i]) if out else (r.at[i], b.at[k]) for r, b in zip(refs, bufs)]
    return [pltpu.make_async_copy(a, b, sems.at[n, k]) for n, (a, b) in enumerate(ends)]


def begin(copies):
    for copy in copies:
        copy.start()


def finish(copies):
    for copy in copies:
        copy.wait()


def gather_kernel(
    counts, slab, relations, idx, theirs,
    heads, rels, weights, own_heads, own_rels, own_tails, marks, rel_marks, rel_wide,
):
    _, _, near, every = place(counts, idx.shape[0])
    widen(relations, rel_wide)

    def own_step(i):
        lidx, ridx, relx, _ = columns(i, 0, 0, (idx, None))
        mark(lidx, marks, slice(0, lidx.shape[1]))
        mark(relx, rel_marks, slice(0, relx.shape[1]))
        own_heads[i] = nn(slab[...], marks[...]).astype(BF16)
        own_rels[i] = nn(rel_wide[...], rel_marks[...]).astype(BF16)
        mark(ridx, marks, slice(0, ridx.shape[1]))
        own_tails[i] = nn(slab[...], marks[...]).astype(BF16)

    repeat(0, near[0], own_step)

    def step(i):
        lidx, _, relx, nidx = columns(i, near[1], 1, (idx, theirs))
        weights[i] = row_counts(nidx, slab.shape[1])
        mark(lidx, marks, slice(0, lidx.shape[1]))
        mark(relx, rel_marks, slice(0, relx.shape[1]))
        heads[i] = nn(slab[...], marks[...]).astype(BF16)
        rels[i] = nn(rel_wide[...], rel_marks[...]).astype(BF16)

    repeat(0, every[1], step)


def own_kernel(
    counts, slab, idx, heads, rels, tails,
    keep, give, rel_total, own, marks, rel_marks, neg, head, rel, tail, sems,
):
    side, _, near, _ = place(counts, idx.shape[0])
    last = near[0]

    def fetch(i):
        return streams((heads, rels, tails), (head, rel, tail), sems, i)

    @pl.when(last >= 1)
    def _():
        begin(fetch(0))

    own[...] = jnp.zeros_like(own)
    rel_total[...] = jnp.zeros_like(rel_total)

    def step(i):
        @pl.when(i + 1 < last)
        def _():
            begin(fetch(i + 1))

        def gathered():
            finish(fetch(i))
            return [buf[lax.rem(i, 2)] for buf in (head, rel, tail)]

        own_slot(i, slab, idx, own, rel_total, marks, rel_marks, neg, gathered)

    repeat(0, last, step)
    middle = keep.shape[1]

    @pl.when(side == 0)
    def _():
        keep[...] = own[:, :middle]
        give[...] = own[:, middle:]

    @pl.when(side != 0)
    def _():
        keep[...] = own[:, middle:]
        give[...] = own[:, :middle]


def right_kernel(
    counts, pieces, idx, theirs, weights, heads, rels,
    other_pieces, pos_grads, right, tails, negs, other, marks, head, rel, tail, neg, in_sems, out_sems,
):
    side, _, near, every = place(counts, idx.shape[0])
    mine, total = near[1], every[1]

    def fetch(i):
        return streams((heads, rels), (head, rel), in_sems, i)

    def away(i):
        return streams((tails, negs), (tail, neg), out_sems, i, out=True)

    @pl.when(total >= 1)
    def _():
        begin(fetch(0))

    other[...] = jnp.zeros_like(other)
    count = len(SLAB_STARTS)
    for j in range(pieces.shape[0]):
        lane, start = (j // count) * LANES, SLAB_STARTS[j % count]
        right[start : start + SLAB_WINDOW, lane : lane + LANES] = pieces[j]
    rows = right.shape[1]
    off = side * (rows // 2)

    def step(i):
        @pl.when(i + 1 < total)
        def _():
            begin(fetch(i + 1))

        @pl.when(i >= 2)
        def _():
            finish(away(i - 2))

        k = lax.rem(i, 2)
        _, ridx, _, nidx = columns(i, mine, 1, (idx, theirs))
        mark(ridx, marks, slice(0, ridx.shape[1]))
        t = nn(right[...], marks[...])
        tail[k] = t.astype(BF16)
        finish(fetch(i))
        query = product(head[k].astype(F32), rel[k].astype(F32))
        pos_grad = -sigmoid(-jnp.sum(query * t, axis=0, keepdims=True))
        pos_grads[i] = pos_grad
        query_low = query.astype(BF16)
        now = neg.at[k]
        negative_terms(query_low, right, now, nidx.shape[1])
        begin(away(i))
        high, low = split(pos_grad * query)
        for to, at in halves(off, rows):
            other[:, to] += nt(high, marks[at, :]) + nt(low, marks[at, :]) + nt(query_low, now[at, :]) * weights[i, :, at]

    repeat(0, total, step)
    count = len(GRAD_STARTS)
    for j in range(other_pieces.shape[0]):
        lane, start = (j // count) * LANES, GRAD_STARTS[j % count]
        other_pieces[j] = other[start : start + GRAD_WINDOW, lane : lane + LANES]

    @pl.when(total >= 2)
    def _():
        finish(away(total - 2))

    @pl.when(total >= 1)
    def _():
        finish(away(total - 1))


def left_steps(first, last, side, mine, idx, saved, own, rel_total, marks, rel_marks, bufs, sems):
    weights, pos_grads, right, *refs = saved
    rows = right.shape[1]
    off = side * (rows // 2)

    def fetch(i):
        return streams(refs, bufs, sems, i)

    @pl.when(first < last)
    def _():
        begin(fetch(first))

    def step(i):
        @pl.when(i + 1 < last)
        def _():
            begin(fetch(i + 1))

        k = lax.rem(i, 2)
        lidx, _, relx, _ = columns(i, mine, 1, idx)
        mark(lidx, marks, slice(0, lidx.shape[1]))
        finish(fetch(i))
        rel, tail, neg = [buf[k] for buf in bufs[:3]]
        query_grad = query_gradient(pos_grads[i], tail.astype(F32), right, weights[i], neg)
        high, low = split(conjugate(query_grad, rel.astype(F32)))
        for to, at in halves(off, rows):
            own[:, to] += nt(high, marks[at, :]) + nt(low, marks[at, :])
        if rel_total is not None:
            mark(relx, rel_marks, slice(0, relx.shape[1]))
            add_relations(conjugate(query_grad, bufs[3][k].astype(F32)), rel_marks, rel_total)

    repeat(first, last, step)


def left_kernel(
    counts, idx, theirs, weights, pos_grads, right, rels, tails, negs, heads, far_own, rel_in,
    own, keep, give, rel_total, marks, rel_marks, rel, tail, neg, head, sems,
):
    side, core, near, _ = place(counts, idx.shape[0])
    own[...] = jnp.zeros_like(own)
    rel_total[...] = rel_in[...]
    left_steps(
        0, near[1], side, near[1], (idx, theirs), (weights, pos_grads, right, rels, tails, negs, heads),
        own, rel_total, marks, rel_marks, (rel, tail, neg, head), sems,
    )
    half = rel_total.shape[0] // 2
    lanes = rel_total.shape[1] // LANES

    def cut(out, first):
        for j in range(lanes):
            out[j * half : (j + 1) * half, :] = rel_total[first : first + half, j * LANES : (j + 1) * LANES]
        out[lanes * half :, :] = jnp.zeros((out.shape[0] - lanes * half, LANES), F32)

    @pl.when(core == 0)
    def _():
        cut(keep, 0)
        cut(give, half)

    @pl.when(core != 0)
    def _():
        cut(keep, half)
        cut(give, 0)


def rest_kernel(
    counts, idx, theirs, weights, pos_grads, right, rels, tails, negs, own_in, near_own, far_own, own, marks, rel, tail, neg, sems,
):
    side, _, near, every = place(counts, idx.shape[0])
    own[...] = own_in[...] + (near_own[...] + far_own[...])
    left_steps(
        near[1], every[1], side, near[1], (idx, theirs), (weights, pos_grads, right, rels, tails, negs),
        own, None, marks, None, (rel, tail, neg), sems,
    )


def cut_kernel(slab, pieces):
    count = len(SLAB_STARTS)
    for j in range(pieces.shape[0]):
        lane, start = (j // count) * LANES, SLAB_STARTS[j % count]
        pieces[j] = slab[start : start + SLAB_WINDOW, lane : lane + LANES]


def take_kernel(matching, held, chosen, sem):
    def step(q, _):
        pltpu.make_async_copy(held.at[matching[q]], chosen.at[q], sem).start()
        return 0

    lax.fori_loop(0, held.shape[0], step, 0)
    pltpu.make_async_copy(held, chosen, sem).wait()


def put_kernel(matching, held, chosen, sem):
    def step(q, _):
        pltpu.make_async_copy(held.at[q], chosen.at[matching[q]], sem).start()
        return 0

    lax.fori_loop(0, held.shape[0], step, 0)
    pltpu.make_async_copy(held, chosen, sem).wait()


def add_kernel(own, pieces, first, second):
    count, cut = len(GRAD_STARTS), first.shape[0]
    for j in range(pieces.shape[0]):
        start, lane = GRAD_STARTS[j % count], (j // count) * LANES
        lanes = slice(lane, lane + LANES)
        total = own[start : start + GRAD_WINDOW, lanes] + pieces[j]
        here = max(0, min(cut - start, GRAD_WINDOW))
        if here:
            first[start : start + here, lanes] = total[:here]
        if here < GRAD_WINDOW:
            second[start + here - cut : start + GRAD_WINDOW - cut, lanes] = total[here:]


def write(parts, sems):
    copies = [pltpu.make_async_copy(a, b, sems.at[n, 0]) for n, (a, b) in enumerate(parts)]
    begin(copies)
    finish(copies)


def join_kernel(first, second, far, out, sems):
    side = lax.axis_index("edge")
    middle, cut = first.shape[1], first.shape[0]

    def put(near, away):
        write([(first, out.at[:cut, near]), (second, out.at[cut:, near]), (far, out.at[:cut, away])], sems)

    @pl.when(side == 0)
    def _():
        put(slice(0, middle), slice(middle, 2 * middle))

    @pl.when(side != 0)
    def _():
        put(slice(middle, 2 * middle), slice(0, middle))


def last_kernel(begun, far, out, sems):
    side = lax.axis_index("edge")
    middle, cut = far.shape[1], out.shape[0] - far.shape[0]

    @pl.when(side == 0)
    def _():
        write([(far, out.at[cut:, middle:])], sems)

    @pl.when(side != 0)
    def _():
        write([(far, out.at[cut:, :middle])], sems)


def pair_kernel(keep, got, out):
    for j in range(out.shape[0]):
        at = slice(j * REL_WINDOW, (j + 1) * REL_WINDOW)
        out[j] = keep[at, :] + got[at, :]


def sum_kernel(held, out):
    total = held[0]
    for j in range(1, held.shape[0]):
        total = total + held[j]
    out[...] = total


def spread_kernel(a, b, c, d, out):
    total = (a[...] + b[...]) + (c[...] + d[...])
    for j in range(out.shape[0]):
        out[j] = total


def close_kernel(mine, theirs, out):
    core = lax.axis_index("dom") % 2
    half, rels = out.shape[0] // 2, out.shape[1]

    def put(ref, first):
        for j in range(-(-rels // LANES)):
            lanes = min(LANES, rels - j * LANES)
            out[first : first + half, j * LANES : j * LANES + lanes] = ref[j * half : (j + 1) * half, :lanes]

    @pl.when(core == 0)
    def _():
        put(mine, 0)
        put(theirs, half)

    @pl.when(core != 0)
    def _():
        put(mine, half)
        put(theirs, 0)


def call(kernel, outs, specs, scratch, *args, flops=0, moved=0, out_specs=None, aliases={}):
    return pl.pallas_call(
        kernel,
        out_shape=outs,
        in_specs=specs,
        out_specs=jax.tree.map(lambda _: VM, outs) if out_specs is None else out_specs,
        scratch_shapes=scratch,
        compiler_params=PARAMS,
        input_output_aliases=aliases,
        cost_estimate=pl.CostEstimate(flops=flops, bytes_accessed=moved, transcendentals=0),
    )(*args)


def shape(dims, kind=F32):
    return jax.ShapeDtypeStruct(dims, kind)


def body(entities, relations, matching, group_counts, left_rows, right_rows, relation_ids, negative_rows):
    parts = lax.axis_size("dom")
    rows, width = entities.shape
    half_slots, edges = left_rows.shape[2:]
    slots = 2 * half_slots
    rels = relations.shape[0]
    padded = -(-rels // LANES) * LANES
    middle = rows // 2
    swap = [(0, 1), (1, 0)]
    plane = 2 * REL_RING
    cores = [(i, i ^ 1) for i in range(parts)]
    planes = [(i, (i + plane) % parts) for i in range(parts)]
    corners = [(2 * i + e, 2 * ((i + plane) % parts) + 1 - e) for i in range(parts) for e in range(2)]
    rings = [[z + 2 * k + c for k in range(REL_RING)] for z in range(0, parts, plane) for c in range(2)]

    def exchange(x, groups=None):
        return lax.all_to_all(x, "dom", split_axis=0, concat_axis=0, tiled=True, axis_index_groups=groups)

    packed = jnp.concatenate(
        [jnp.swapaxes(ref[0], 0, 1) for ref in (left_rows, right_rows, relation_ids, negative_rows)], axis=2
    )
    idx = (packed, lax.ppermute(packed, "edge", swap))
    slab = entities.T
    relations = relations.T
    pieces = call(cut_kernel, shape((parts, SLAB_WINDOW, LANES), BF16), [VM], [], slab)
    pieces, idx = lax.optimization_barrier((pieces, idx))
    held = exchange(pieces)

    def mem(rows_, lanes, kind=BF16):
        return pltpu.VMEM((rows_, lanes), kind)

    one_mark, two_marks, neg = mem(rows, edges), mem(rows, 2 * edges), mem(rows, edges)
    rel_marks, rel_wide = mem(padded, edges), mem(width, padded)
    two_neg = pltpu.VMEM((2, rows, edges), BF16)
    two_wide = pltpu.VMEM((2, width, edges), BF16)
    sem = pltpu.SemaphoreType.DMA

    def sems(count):
        return sem((count, 2))

    unit = 2 * width * rows * edges
    own_shape, rel_shape = shape((width, middle)), shape((width, padded))
    gathered = shape((slots, width, edges), BF16)

    near_gathered = shape((half_slots, width, edges), BF16)
    heads, rel_rows, weights, *own_rows = call(
        gather_kernel, (gathered, gathered, shape((slots, 1, rows))) + (near_gathered,) * 3,
        [SM] + [VM] * 4, [one_mark, rel_marks, rel_wide],
        group_counts, slab, relations, *idx, flops=22 * unit,
    )
    held, heads = lax.optimization_barrier((held, heads))
    chosen = call(take_kernel, shape(held.shape, BF16), [SM, HB], [sem], matching, held)
    partner = exchange(chosen)
    keep, give, rel_total = call(
        own_kernel, (own_shape, own_shape, rel_shape), [SM] + [VM] * 2 + [HB] * 3,
        [mem(width, rows, F32), two_marks, rel_marks, neg, two_wide, two_wide, two_wide, sems(3)],
        group_counts, slab, packed, *own_rows, flops=32 * unit,
    )
    got = lax.ppermute(give, "edge", swap)
    other, pos_grads, right, tails, negs = call(
        right_kernel,
        (
            shape((parts, GRAD_WINDOW, LANES)),
            shape((slots, 1, edges)),
            shape((width, rows), BF16),
            gathered,
            shape((slots, rows, edges), BF16),
        ),
        [SM] + [VM] * 4 + [HB] * 2,
        [mem(width, middle, F32), one_mark, two_wide, two_wide, two_wide, two_neg, sems(2), sems(2)],
        group_counts, partner, *idx, weights, heads, rel_rows,
        flops=30 * unit, out_specs=(VM, VM, VM, HB, HB),
    )
    grad_held = exchange(other)
    rel_flat = shape((REL_RING * REL_WINDOW, LANES))
    saved = (weights, pos_grads, right, rel_rows, tails, negs)
    own, rel_keep, rel_give = call(
        left_kernel, (own_shape, rel_flat, rel_flat), [SM] + [VM] * 5 + [HB] * 5 + [VM],
        [mem(width, padded, F32), one_mark, rel_marks, two_wide, two_wide, two_neg, two_wide, sems(4)],
        group_counts, *idx, *saved, heads, got, rel_total, flops=20 * unit,
    )
    rel_got = lax.ppermute(rel_give, "dom", cores)
    grad_chosen = call(put_kernel, shape(grad_held.shape), [SM, VM], [sem], matching, grad_held, out_specs=HB)
    grad_pieces = exchange(grad_chosen)
    rel_keep, own, grad_chosen = lax.optimization_barrier((rel_keep, own, grad_chosen))
    rel_pieces = call(pair_kernel, shape((REL_RING, REL_WINDOW, LANES)), [VM, VM], [], rel_keep, rel_got)
    own = call(
        rest_kernel, own_shape, [SM] + [VM] * 5 + [HB] * 3 + [VM] * 3, [one_mark, two_wide, two_wide, two_neg, sems(3)],
        group_counts, *idx, *saved, own, keep, got, flops=15 * unit,
    )
    own, grad_pieces, rel_pieces = lax.optimization_barrier((own, grad_pieces, rel_pieces))
    cut = EARLY_ROWS
    half_shapes = (shape((cut, middle)), shape((width - cut, middle)))
    first, second = call(add_kernel, half_shapes, [VM] * 2, [], own, grad_pieces)
    far = [lax.ppermute(first, "edge", swap), None]
    rel_pieces, second = lax.optimization_barrier((rel_pieces, second))
    rel_held = exchange(rel_pieces, rings)
    whole = shape((width, rows))
    total = call(join_kernel, whole, [VM] * 3, [sems(3)], first, second, far[0], out_specs=HB, flops=60 * unit)
    rel_held, total = lax.optimization_barrier((rel_held, total))
    rel_sum = call(sum_kernel, shape((REL_WINDOW, LANES)), [VM], [], rel_held)
    rel_sums = [rel_sum, lax.ppermute(rel_sum, "dom", planes), lax.ppermute(rel_sum, "edge", swap)]
    rel_sums += [lax.ppermute(rel_sum, ("dom", "edge"), corners)]
    second, rel_sums = lax.optimization_barrier((second, rel_sums))
    far[1] = lax.ppermute(second, "edge", swap)
    rel_full = call(spread_kernel, shape(rel_pieces.shape), [VM] * 4, [], *rel_sums)
    rel_mine = exchange(rel_full, rings).reshape(rel_flat.shape)
    total = call(
        last_kernel, whole, [HB, VM], [sems(1)], total, far[1], out_specs=HB, aliases={0: 0}, flops=60 * unit
    )
    rel_mine, total = lax.optimization_barrier((rel_mine, total))
    rel_far = lax.ppermute(rel_mine, "dom", cores)
    relation_grad = call(close_kernel, shape((width, rels)), [VM, VM], [], rel_mine, rel_far)
    return total.T, relation_grad.T


def solution(mesh):
    placed = (
        P("dom", None),
        P(),
        P(),
        P("dom", None),
        P("dom", None, "edge", None),
        P("dom", None, "edge", None),
        P("dom", None, "edge", None),
        P("dom", None, "edge", None),
    )
    return jax.shard_map(
        body, mesh=mesh, in_specs=placed, out_specs=(P("dom", None), P()), check_vma=False
    )
```

```python
import jax
import jax.numpy as jnp
from jax import lax
from jax.experimental import pallas as pl
from jax.experimental.pallas import tpu as pltpu
from jax.sharding import PartitionSpec as P

F32 = jnp.float32
BF16 = jnp.bfloat16
CHUNK = 512
VM = pl.BlockSpec(memory_space=pltpu.VMEM)
SM = pl.BlockSpec(memory_space=pltpu.SMEM)
HB = pl.BlockSpec(memory_space=pl.ANY)
PARAMS = pltpu.CompilerParams(vmem_limit_bytes=63 * 2**20)

LANES = 128
SLAB_WINDOW = 112
SLAB_STARTS = (0, 96, 192, 288)
GRAD_WINDOW = 56
GRAD_STARTS = (0, 56, 112, 168, 224, 280, 336, 344)
EARLY_ROWS = 168
REL_WINDOW = 144
REL_RING = 16


def nn(a, b):
    return lax.dot_general(a, b, (((1,), (0,)), ((), ())), preferred_element_type=F32)


def nt(a, b):
    return lax.dot_general(a, b, (((1,), (1,)), ((), ())), preferred_element_type=F32)


def tn(a, b):
    return lax.dot_general(a, b, (((0,), (0,)), ((), ())), preferred_element_type=F32)


def one_hot(idx, first, count):
    rows = lax.broadcasted_iota(jnp.int16, (count, idx.shape[1]), 0) + jnp.int16(first)
    return jnp.where(rows == idx.astype(jnp.int16), jnp.ones((), BF16), jnp.zeros((), BF16))


def mark(idx, out, lanes):
    for c in range(0, out.shape[0], LANES):
        out[c : c + LANES, lanes] = one_hot(idx, c, LANES)


def row_counts(idx, rows):
    high = one_hot(idx >> 7, 0, rows // LANES)
    low = one_hot(idx & (LANES - 1), 0, LANES)
    table = nt(high, low)
    return jnp.concatenate([table[i : i + 1, :] for i in range(rows // LANES)], axis=1)


def split(x):
    high = x.astype(BF16)
    return high, (x - high.astype(F32)).astype(BF16)


def sigmoid(x):
    return 1.0 / (1.0 + jnp.exp(-x))


def product(h, r):
    half = h.shape[0] // 2
    a, b, c, d = h[:half], h[half:], r[:half], r[half:]
    return jnp.concatenate([a * c - b * d, a * d + b * c], axis=0)


def conjugate(grad, r):
    half = grad.shape[0] // 2
    a, b, c, d = grad[:half], grad[half:], r[:half], r[half:]
    return jnp.concatenate([a * c + b * d, b * c - a * d], axis=0)


def columns(position, mine, bucket, idx):
    ours, theirs = idx
    slots = ours.shape[0]
    near = ours[jnp.minimum(position, slots - 1)]
    if theirs is None:
        row = near
    else:
        row = jnp.where(position < mine, near, theirs[jnp.clip(position - mine, 0, slots - 1)])
    row = row[bucket : bucket + 1]
    edges = row.shape[1] // 5
    return row[:, :edges], row[:, edges : 2 * edges], row[:, 2 * edges : 3 * edges], row[:, 3 * edges :]


def halves(off, rows):
    for c in range(0, rows // 2, CHUNK):
        yield slice(c, c + CHUNK), pl.ds(pl.multiple_of(off + c, CHUNK), CHUNK)


def negative_terms(query_low, slab, neg, negatives):
    for c in range(0, slab.shape[1], CHUNK):
        scores = tn(slab[:, c : c + CHUNK], query_low)
        neg[c : c + CHUNK, :] = (sigmoid(scores) * (1.0 / negatives)).astype(BF16)


def query_gradient(pos_grad, t, right, counts, neg):
    high, low = split(right[...].astype(F32) * counts)
    return pos_grad * t + nn(high, neg) + nn(low, neg)


def add_relations(grad, rel_marks, rel_total):
    high, low = split(grad)
    rel_total[...] += nt(high, rel_marks[...]) + nt(low, rel_marks[...])


def own_slot(position, slab, idx, own, marks, neg, gathered, keep_relation):
    lidx, ridx, _, nidx = columns(position, 0, 0, (idx, None))
    edges, negatives = lidx.shape[1], nidx.shape[1]
    rows = slab.shape[1]
    mark(lidx, marks, slice(0, edges))
    mark(ridx, marks, slice(edges, 2 * edges))
    h, rel, t = [x.astype(F32) for x in gathered()]
    query = product(h, rel)
    pos_grad = -sigmoid(-jnp.sum(query * t, axis=0, keepdims=True))
    query_low = query.astype(BF16)
    counts = row_counts(nidx, rows)
    negative_terms(query_low, slab, neg, negatives)
    query_grad = query_gradient(pos_grad, t, slab, counts, neg[...])
    head_high, head_low = split(conjugate(query_grad, rel))
    tail_high, tail_low = split(pos_grad * query)
    both_high = jnp.concatenate([head_high, tail_high], axis=1)
    both_low = jnp.concatenate([head_low, tail_low], axis=1)
    for c in range(0, rows, CHUNK):
        at = slice(c, c + CHUNK)
        own[:, at] += (
            nt(both_high, marks[at, :]) + nt(both_low, marks[at, :]) + nt(query_low, neg[at, :]) * counts[:, at]
        )
    keep_relation(*split(conjugate(query_grad, h)))


def widen(relations, rel_wide):
    rels = relations.shape[1]
    rel_wide[:, rels // LANES * LANES :] = jnp.zeros((rel_wide.shape[0], LANES), BF16)
    rel_wide[:, :rels] = relations[...]


def repeat(first, last, step):
    def run(i, _):
        step(i)
        return 0

    lax.fori_loop(first, last, run, 0)


def place(counts, slots):
    side = lax.axis_index("edge").astype(jnp.int32)
    core = (lax.axis_index("dom") % 2).astype(jnp.int32)
    every = [jnp.clip(counts[0, b], 0, 2 * slots) for b in range(2)]
    near = [jnp.clip(c - side * slots, 0, slots) for c in every]
    return side, core, near, every


def streams(refs, bufs, sems, i, out=False):
    k = lax.rem(i, 2)
    ends = [(b.at[k], r.at[i]) if out else (r.at[i], b.at[k]) for r, b in zip(refs, bufs)]
    return [pltpu.make_async_copy(a, b, sems.at[n, k]) for n, (a, b) in enumerate(ends)]


def begin(copies):
    for copy in copies:
        copy.start()


def finish(copies):
    for copy in copies:
        copy.wait()


def gather_kernel(
    counts, slab, relations, idx, theirs,
    heads, rels, weights, own_heads, own_rels, own_tails, marks, rel_marks, rel_wide,
):
    _, _, near, every = place(counts, idx.shape[0])
    widen(relations, rel_wide)

    def own_step(i):
        lidx, ridx, relx, _ = columns(i, 0, 0, (idx, None))
        mark(lidx, marks, slice(0, lidx.shape[1]))
        mark(relx, rel_marks, slice(0, relx.shape[1]))
        own_heads[i] = nn(slab[...], marks[...]).astype(BF16)
        own_rels[i] = nn(rel_wide[...], rel_marks[...]).astype(BF16)
        mark(ridx, marks, slice(0, ridx.shape[1]))
        own_tails[i] = nn(slab[...], marks[...]).astype(BF16)

    repeat(0, near[0], own_step)

    def step(i):
        lidx, _, relx, nidx = columns(i, near[1], 1, (idx, theirs))
        weights[i] = row_counts(nidx, slab.shape[1])
        mark(lidx, marks, slice(0, lidx.shape[1]))
        mark(relx, rel_marks, slice(0, relx.shape[1]))
        heads[i] = nn(slab[...], marks[...]).astype(BF16)
        rels[i] = nn(rel_wide[...], rel_marks[...]).astype(BF16)

    repeat(0, every[1], step)


def own_kernel(
    counts, slab, idx, heads, rels, tails,
    keep, give, rel_highs, rel_lows, own, marks, neg, head, rel, tail, rel_high, rel_low, sems, out_sems,
):
    side, _, near, _ = place(counts, idx.shape[0])
    last = near[0]

    def fetch(i):
        return streams((heads, rels, tails), (head, rel, tail), sems, i)

    def away(i):
        return streams((rel_highs, rel_lows), (rel_high, rel_low), out_sems, i, out=True)

    @pl.when(last >= 1)
    def _():
        begin(fetch(0))

    own[...] = jnp.zeros_like(own)

    def step(i):
        @pl.when(i + 1 < last)
        def _():
            begin(fetch(i + 1))

        def gathered():
            finish(fetch(i))
            return [buf[lax.rem(i, 2)] for buf in (head, rel, tail)]

        def keep_relation(high, low):
            k = lax.rem(i, 2)

            @pl.when(i >= 2)
            def _():
                finish(away(i - 2))

            rel_high[k] = high
            rel_low[k] = low
            begin(away(i))

        own_slot(i, slab, idx, own, marks, neg, gathered, keep_relation)

    repeat(0, last, step)

    @pl.when(last >= 2)
    def _():
        finish(away(last - 2))

    @pl.when(last >= 1)
    def _():
        finish(away(last - 1))

    middle = keep.shape[1]

    @pl.when(side == 0)
    def _():
        keep[...] = own[:, :middle]
        give[...] = own[:, middle:]

    @pl.when(side != 0)
    def _():
        keep[...] = own[:, middle:]
        give[...] = own[:, :middle]


def right_kernel(
    counts, pieces, idx, theirs, weights, heads, rels,
    other_pieces, pos_grads, right, tails, negs, other, marks, head, rel, tail, neg, in_sems, out_sems,
):
    side, _, near, every = place(counts, idx.shape[0])
    mine, total = near[1], every[1]

    def fetch(i):
        return streams((heads, rels), (head, rel), in_sems, i)

    def away(i):
        return streams((tails, negs), (tail, neg), out_sems, i, out=True)

    @pl.when(total >= 1)
    def _():
        begin(fetch(0))

    other[...] = jnp.zeros_like(other)
    count = len(SLAB_STARTS)
    for j in range(pieces.shape[0]):
        lane, start = (j // count) * LANES, SLAB_STARTS[j % count]
        right[start : start + SLAB_WINDOW, lane : lane + LANES] = pieces[j]
    rows = right.shape[1]
    off = side * (rows // 2)

    def step(i):
        @pl.when(i + 1 < total)
        def _():
            begin(fetch(i + 1))

        @pl.when(i >= 2)
        def _():
            finish(away(i - 2))

        k = lax.rem(i, 2)
        _, ridx, _, nidx = columns(i, mine, 1, (idx, theirs))
        mark(ridx, marks, slice(0, ridx.shape[1]))
        t = nn(right[...], marks[...])
        tail[k] = t.astype(BF16)
        finish(fetch(i))
        query = product(head[k].astype(F32), rel[k].astype(F32))
        pos_grad = -sigmoid(-jnp.sum(query * t, axis=0, keepdims=True))
        pos_grads[i] = pos_grad
        query_low = query.astype(BF16)
        now = neg.at[k]
        negative_terms(query_low, right, now, nidx.shape[1])
        begin(away(i))
        high, low = split(pos_grad * query)
        for to, at in halves(off, rows):
            other[:, to] += nt(high, marks[at, :]) + nt(low, marks[at, :]) + nt(query_low, now[at, :]) * weights[i, :, at]

    repeat(0, total, step)
    count = len(GRAD_STARTS)
    for j in range(other_pieces.shape[0]):
        lane, start = (j // count) * LANES, GRAD_STARTS[j % count]
        other_pieces[j] = other[start : start + GRAD_WINDOW, lane : lane + LANES]

    @pl.when(total >= 2)
    def _():
        finish(away(total - 2))

    @pl.when(total >= 1)
    def _():
        finish(away(total - 1))


def left_steps(first, last, side, mine, idx, saved, own, rel_total, marks, rel_marks, bufs, sems):
    weights, pos_grads, right, *refs = saved
    rows = right.shape[1]
    off = side * (rows // 2)

    def fetch(i):
        return streams(refs, bufs, sems, i)

    @pl.when(first < last)
    def _():
        begin(fetch(first))

    def step(i):
        @pl.when(i + 1 < last)
        def _():
            begin(fetch(i + 1))

        k = lax.rem(i, 2)
        lidx, _, relx, _ = columns(i, mine, 1, idx)
        mark(lidx, marks, slice(0, lidx.shape[1]))
        finish(fetch(i))
        rel, tail, neg = [buf[k] for buf in bufs[:3]]
        query_grad = query_gradient(pos_grads[i], tail.astype(F32), right, weights[i], neg)
        high, low = split(conjugate(query_grad, rel.astype(F32)))
        for to, at in halves(off, rows):
            own[:, to] += nt(high, marks[at, :]) + nt(low, marks[at, :])
        if rel_total is not None:
            mark(relx, rel_marks, slice(0, relx.shape[1]))
            add_relations(conjugate(query_grad, bufs[3][k].astype(F32)), rel_marks, rel_total)

    repeat(first, last, step)


def left_kernel(
    counts, idx, theirs, weights, pos_grads, right, rels, tails, negs, heads, far_own, rel_highs, rel_lows,
    own, keep, give, rel_total, marks, rel_marks, rel, tail, neg, head, sems, rel_sems,
):
    side, core, near, _ = place(counts, idx.shape[0])

    def fetch(i):
        return streams((rel_highs, rel_lows), (rel, head), rel_sems, i)

    @pl.when(near[0] >= 1)
    def _():
        begin(fetch(0))

    own[...] = jnp.zeros_like(own)
    rel_total[...] = jnp.zeros_like(rel_total)

    def step(i):
        @pl.when(i + 1 < near[0])
        def _():
            begin(fetch(i + 1))

        k = lax.rem(i, 2)
        relx = columns(i, 0, 0, (idx, None))[2]
        mark(relx, rel_marks, slice(0, relx.shape[1]))
        finish(fetch(i))
        rel_total[...] += nt(rel[k], rel_marks[...]) + nt(head[k], rel_marks[...])

    repeat(0, near[0], step)
    left_steps(
        0, near[1], side, near[1], (idx, theirs), (weights, pos_grads, right, rels, tails, negs, heads),
        own, rel_total, marks, rel_marks, (rel, tail, neg, head), sems,
    )
    half = rel_total.shape[0] // 2
    lanes = rel_total.shape[1] // LANES

    def cut(out, first):
        for j in range(lanes):
            out[j * half : (j + 1) * half, :] = rel_total[first : first + half, j * LANES : (j + 1) * LANES]
        out[lanes * half :, :] = jnp.zeros((out.shape[0] - lanes * half, LANES), F32)

    @pl.when(core == 0)
    def _():
        cut(keep, 0)
        cut(give, half)

    @pl.when(core != 0)
    def _():
        cut(keep, half)
        cut(give, 0)


def rest_kernel(
    counts, idx, theirs, weights, pos_grads, right, rels, tails, negs, own_in, near_own, far_own, own, marks, rel, tail, neg, sems,
):
    side, _, near, every = place(counts, idx.shape[0])
    own[...] = own_in[...] + (near_own[...] + far_own[...])
    left_steps(
        near[1], every[1], side, near[1], (idx, theirs), (weights, pos_grads, right, rels, tails, negs),
        own, None, marks, None, (rel, tail, neg), sems,
    )


def cut_kernel(slab, pieces):
    count = len(SLAB_STARTS)
    for j in range(pieces.shape[0]):
        lane, start = (j // count) * LANES, SLAB_STARTS[j % count]
        pieces[j] = slab[start : start + SLAB_WINDOW, lane : lane + LANES]


def take_kernel(matching, held, chosen, sem):
    def step(q, _):
        pltpu.make_async_copy(held.at[matching[q]], chosen.at[q], sem).start()
        return 0

    lax.fori_loop(0, held.shape[0], step, 0)
    pltpu.make_async_copy(held, chosen, sem).wait()


def put_kernel(matching, held, chosen, sem):
    def step(q, _):
        pltpu.make_async_copy(held.at[q], chosen.at[matching[q]], sem).start()
        return 0

    lax.fori_loop(0, held.shape[0], step, 0)
    pltpu.make_async_copy(held, chosen, sem).wait()


def add_kernel(own, pieces, first, second):
    count, cut = len(GRAD_STARTS), first.shape[0]
    for j in range(pieces.shape[0]):
        start, lane = GRAD_STARTS[j % count], (j // count) * LANES
        lanes = slice(lane, lane + LANES)
        total = own[start : start + GRAD_WINDOW, lanes] + pieces[j]
        here = max(0, min(cut - start, GRAD_WINDOW))
        if here:
            first[start : start + here, lanes] = total[:here]
        if here < GRAD_WINDOW:
            second[start + here - cut : start + GRAD_WINDOW - cut, lanes] = total[here:]


def write(parts, sems):
    copies = [pltpu.make_async_copy(a, b, sems.at[n, 0]) for n, (a, b) in enumerate(parts)]
    begin(copies)
    finish(copies)


def join_kernel(first, second, far, out, sems):
    side = lax.axis_index("edge")
    middle, cut = first.shape[1], first.shape[0]

    def put(near, away):
        write([(first, out.at[:cut, near]), (second, out.at[cut:, near]), (far, out.at[:cut, away])], sems)

    @pl.when(side == 0)
    def _():
        put(slice(0, middle), slice(middle, 2 * middle))

    @pl.when(side != 0)
    def _():
        put(slice(middle, 2 * middle), slice(0, middle))


def last_kernel(begun, far, out, sems):
    side = lax.axis_index("edge")
    middle, cut = far.shape[1], out.shape[0] - far.shape[0]

    @pl.when(side == 0)
    def _():
        write([(far, out.at[cut:, middle:])], sems)

    @pl.when(side != 0)
    def _():
        write([(far, out.at[cut:, :middle])], sems)


def pair_kernel(keep, got, out):
    for j in range(out.shape[0]):
        at = slice(j * REL_WINDOW, (j + 1) * REL_WINDOW)
        out[j] = keep[at, :] + got[at, :]


def sum_kernel(held, out):
    total = held[0]
    for j in range(1, held.shape[0]):
        total = total + held[j]
    out[...] = total


def spread_kernel(a, b, c, d, out):
    total = (a[...] + b[...]) + (c[...] + d[...])
    for j in range(out.shape[0]):
        out[j] = total


def close_kernel(mine, theirs, out):
    core = lax.axis_index("dom") % 2
    half, rels = out.shape[0] // 2, out.shape[1]

    def put(ref, first):
        for j in range(-(-rels // LANES)):
            lanes = min(LANES, rels - j * LANES)
            out[first : first + half, j * LANES : j * LANES + lanes] = ref[j * half : (j + 1) * half, :lanes]

    @pl.when(core == 0)
    def _():
        put(mine, 0)
        put(theirs, half)

    @pl.when(core != 0)
    def _():
        put(mine, half)
        put(theirs, 0)


def call(kernel, outs, specs, scratch, *args, flops=0, moved=0, out_specs=None, aliases={}):
    return pl.pallas_call(
        kernel,
        out_shape=outs,
        in_specs=specs,
        out_specs=jax.tree.map(lambda _: VM, outs) if out_specs is None else out_specs,
        scratch_shapes=scratch,
        compiler_params=PARAMS,
        input_output_aliases=aliases,
        cost_estimate=pl.CostEstimate(flops=flops, bytes_accessed=moved, transcendentals=0),
    )(*args)


def shape(dims, kind=F32):
    return jax.ShapeDtypeStruct(dims, kind)


def body(entities, relations, matching, group_counts, left_rows, right_rows, relation_ids, negative_rows):
    parts = lax.axis_size("dom")
    rows, width = entities.shape
    half_slots, edges = left_rows.shape[2:]
    slots = 2 * half_slots
    rels = relations.shape[0]
    padded = -(-rels // LANES) * LANES
    middle = rows // 2
    swap = [(0, 1), (1, 0)]
    plane = 2 * REL_RING
    cores = [(i, i ^ 1) for i in range(parts)]
    planes = [(i, (i + plane) % parts) for i in range(parts)]
    corners = [(2 * i + e, 2 * ((i + plane) % parts) + 1 - e) for i in range(parts) for e in range(2)]
    rings = [[z + 2 * k + c for k in range(REL_RING)] for z in range(0, parts, plane) for c in range(2)]

    def exchange(x, groups=None):
        return lax.all_to_all(x, "dom", split_axis=0, concat_axis=0, tiled=True, axis_index_groups=groups)

    packed = jnp.concatenate(
        [jnp.swapaxes(ref[0], 0, 1) for ref in (left_rows, right_rows, relation_ids, negative_rows)], axis=2
    )
    idx = (packed, lax.ppermute(packed, "edge", swap))
    slab = entities.T
    relations = relations.T
    pieces = call(cut_kernel, shape((parts, SLAB_WINDOW, LANES), BF16), [VM], [], slab)
    pieces, idx = lax.optimization_barrier((pieces, idx))
    held = exchange(pieces)

    def mem(rows_, lanes, kind=BF16):
        return pltpu.VMEM((rows_, lanes), kind)

    one_mark, two_marks, neg = mem(rows, edges), mem(rows, 2 * edges), mem(rows, edges)
    rel_marks, rel_wide = mem(padded, edges), mem(width, padded)
    two_neg = pltpu.VMEM((2, rows, edges), BF16)
    two_wide = pltpu.VMEM((2, width, edges), BF16)
    sem = pltpu.SemaphoreType.DMA

    def sems(count):
        return sem((count, 2))

    unit = 2 * width * rows * edges
    own_shape, rel_shape = shape((width, middle)), shape((width, padded))
    gathered = shape((slots, width, edges), BF16)

    near_gathered = shape((half_slots, width, edges), BF16)
    heads, rel_rows, weights, *own_rows = call(
        gather_kernel, (gathered, gathered, shape((slots, 1, rows))) + (near_gathered,) * 3,
        [SM] + [VM] * 4, [one_mark, rel_marks, rel_wide],
        group_counts, slab, relations, *idx, flops=22 * unit,
    )
    held, heads = lax.optimization_barrier((held, heads))
    chosen = call(take_kernel, shape(held.shape, BF16), [SM, HB], [sem], matching, held)
    partner = exchange(chosen)
    keep, give, rel_highs, rel_lows = call(
        own_kernel, (own_shape, own_shape, near_gathered, near_gathered), [SM] + [VM] * 2 + [HB] * 3,
        [mem(width, rows, F32), two_marks, neg] + [two_wide] * 5 + [sems(3), sems(2)],
        group_counts, slab, packed, *own_rows, flops=32 * unit, out_specs=(VM, VM, HB, HB),
    )
    got = lax.ppermute(give, "edge", swap)
    other, pos_grads, right, tails, negs = call(
        right_kernel,
        (
            shape((parts, GRAD_WINDOW, LANES)),
            shape((slots, 1, edges)),
            shape((width, rows), BF16),
            gathered,
            shape((slots, rows, edges), BF16),
        ),
        [SM] + [VM] * 4 + [HB] * 2,
        [mem(width, middle, F32), one_mark, two_wide, two_wide, two_wide, two_neg, sems(2), sems(2)],
        group_counts, partner, *idx, weights, heads, rel_rows,
        flops=30 * unit, out_specs=(VM, VM, VM, HB, HB),
    )
    grad_held = exchange(other)
    rel_flat = shape((REL_RING * REL_WINDOW, LANES))
    saved = (weights, pos_grads, right, rel_rows, tails, negs)
    own, rel_keep, rel_give = call(
        left_kernel, (own_shape, rel_flat, rel_flat), [SM] + [VM] * 5 + [HB] * 7,
        [mem(width, padded, F32), one_mark, rel_marks, two_wide, two_wide, two_neg, two_wide, sems(4), sems(2)],
        group_counts, *idx, *saved, heads, got, rel_highs, rel_lows, flops=20 * unit,
    )
    rel_got = lax.ppermute(rel_give, "dom", cores)
    grad_chosen = call(put_kernel, shape(grad_held.shape), [SM, VM], [sem], matching, grad_held, out_specs=HB)
    grad_pieces = exchange(grad_chosen)
    rel_keep, own, grad_chosen = lax.optimization_barrier((rel_keep, own, grad_chosen))
    rel_pieces = call(pair_kernel, shape((REL_RING, REL_WINDOW, LANES)), [VM, VM], [], rel_keep, rel_got)
    own = call(
        rest_kernel, own_shape, [SM] + [VM] * 5 + [HB] * 3 + [VM] * 3, [one_mark, two_wide, two_wide, two_neg, sems(3)],
        group_counts, *idx, *saved, own, keep, got, flops=15 * unit,
    )
    own, grad_pieces, rel_pieces = lax.optimization_barrier((own, grad_pieces, rel_pieces))
    cut = EARLY_ROWS
    half_shapes = (shape((cut, middle)), shape((width - cut, middle)))
    first, second = call(add_kernel, half_shapes, [VM] * 2, [], own, grad_pieces)
    far = [lax.ppermute(first, "edge", swap), None]
    rel_pieces, second = lax.optimization_barrier((rel_pieces, second))
    rel_held = exchange(rel_pieces, rings)
    whole = shape((width, rows))
    total = call(join_kernel, whole, [VM] * 3, [sems(3)], first, second, far[0], out_specs=HB, flops=60 * unit)
    rel_held, total = lax.optimization_barrier((rel_held, total))
    rel_sum = call(sum_kernel, shape((REL_WINDOW, LANES)), [VM], [], rel_held)
    rel_sums = [rel_sum, lax.ppermute(rel_sum, "dom", planes), lax.ppermute(rel_sum, "edge", swap)]
    rel_sums += [lax.ppermute(rel_sum, ("dom", "edge"), corners)]
    second, rel_sums = lax.optimization_barrier((second, rel_sums))
    far[1] = lax.ppermute(second, "edge", swap)
    rel_full = call(spread_kernel, shape(rel_pieces.shape), [VM] * 4, [], *rel_sums)
    rel_mine = exchange(rel_full, rings).reshape(rel_flat.shape)
    total = call(
        last_kernel, whole, [HB, VM], [sems(1)], total, far[1], out_specs=HB, aliases={0: 0}, flops=60 * unit
    )
    rel_mine, total = lax.optimization_barrier((rel_mine, total))
    rel_far = lax.ppermute(rel_mine, "dom", cores)
    relation_grad = call(close_kernel, shape((width, rels)), [VM, VM], [], rel_mine, rel_far)
    return total.T, relation_grad.T


def solution(mesh):
    placed = (
        P("dom", None),
        P(),
        P(),
        P("dom", None),
        P("dom", None, "edge", None),
        P("dom", None, "edge", None),
        P("dom", None, "edge", None),
        P("dom", None, "edge", None),
    )
    return jax.shard_map(
        body, mesh=mesh, in_specs=placed, out_specs=(P("dom", None), P()), check_vma=False
    )
```
